128 devices in a mesh: leaf: 128 (over y, x, z, core).
Axes of the slice: x: 4, y: 4, z: 4, core: 2. Of those that a mesh axis runs over, the one named last changes fastest.
Arguments:
- points: bfloat16 [32, 1048576], P(None, 'leaf'), may hold values from -1 to 1
- rhs: bfloat16 [16, 1048576], P(None, 'leaf'), may hold values from -6 to 6
- basis: bfloat16 [64, 1048576], P(None, 'leaf'), may hold values from -0.375 to 0.375
- transfer_one: bfloat16 [1024, 64, 256], P('leaf'), may hold values from -0.75 to 0.75
- transfer_two: bfloat16 [256, 64, 256], P('leaf'), may hold values from -0.75 to 0.75
- skeleton_one: bfloat16 [32, 65536], P(None, 'leaf'), may hold values from -1 to 1
- skeleton_two: bfloat16 [32, 16384], P(None, 'leaf'), may hold values from -1 to 1
- near_source: int32 [4096, 10], replicated, may hold values from 0 to 4095, as said below
- far_one: int32 [1024, 8], P('leaf'), may hold values from 0 to 1023, as said below
- far_two: int32 [256, 8], P('leaf'), may hold values from 0 to 255, as said below
Outputs:
- potential: bfloat16 [16, 1048576], P(None, 'leaf')
The draws below stay inside these ranges and needn't reach their ends.
Inputs may be any that keep to these rules, and one draw needn't show every extreme that they name: `near_source`: entry 0 of row t is t itself. The rows of the 32 leaves of one device name, of each other device, at most 4 distinct leaves: exactly 4 of each of the two devices whose index differs by one modulo 128, and 1 to 2 of every other device; all other entries name leaves of the row's own device. `far_one`: no row names a cluster of its own device (clusters are spread in order, 8 a device). The rows of one device name, of each other device, at most 2 distinct clusters, exactly 2 of the device whose index is one higher modulo 128; repeats within a row are possible. `far_two`: no row names a cluster of its own device (clusters are spread in order, 2 a device). The rows of one device name, of each other device, at most 2 distinct clusters, exactly 2 of the device whose index is one higher modulo 128; repeats within a row are possible.
All inputs are finite; a program needn't handle non-finite values.
Results may differ from the reference program's by a relative error of at most 0.009.
Values may be sent and summed in bfloat16 or wider, within the bound.
No kernel may reach another device: no remote copies, remote signals or barrier semaphores. Data moves between devices by JAX's collectives and lax.ppermute only.
A program may use at most 128 MiB of HBM per device.

```python
import jax
import jax.numpy as jnp
from jax import lax

DIM = 32
NRHS = 16
RANK = 64
LEAF = 256
NEAR = 10
FAR = 8
CAP = 4
OTHERCAP = 2
FARCAP = 2
LEAF_DEV = 32
PEERS = 128
LEAVES = 4096
POINTS = 1048576
CL_ONE = 1024
CL_TWO = 256


def near_plan(key):
    peer_count = PEERS
    slots = LEAF_DEV * (NEAR - 1)
    key_parts = jax.random.split(key, 4)
    receiver = jnp.arange(peer_count, dtype=jnp.int32)[:, None]
    sender = jnp.arange(peer_count, dtype=jnp.int32)[None, :]
    counts = jax.random.randint(key_parts[0], (peer_count, peer_count), 1, OTHERCAP + 1, dtype=jnp.int32)
    offset = (sender - receiver) % peer_count
    counts = jnp.where(offset == 2, OTHERCAP, counts)
    counts = jnp.where((offset == 1) | (offset == peer_count - 1), CAP, counts)
    counts = jnp.where(offset == 0, 0, counts)
    scores = jax.random.randint(key_parts[1], (peer_count, peer_count, LEAF_DEV), 0, 1 << 20, dtype=jnp.int32)
    scores = scores * LEAF_DEV + jnp.arange(LEAF_DEV, dtype=jnp.int32)
    rank_order = jnp.argsort(scores, axis=-1).astype(jnp.int32)[..., :CAP]
    column = jnp.arange(CAP, dtype=jnp.int32)
    chosen = jnp.where(column < counts[..., None], rank_order, LEAF_DEV)
    wanted = jnp.where(chosen < LEAF_DEV, sender[..., None] * LEAF_DEV + chosen, 0).reshape(peer_count, peer_count * CAP)
    status = jnp.where(chosen < LEAF_DEV, 0, 2).reshape(peer_count, peer_count * CAP).astype(jnp.int32)
    filler = receiver * LEAF_DEV + jax.random.randint(key_parts[2], (peer_count, slots), 0, LEAF_DEV, dtype=jnp.int32)
    source_pool = jnp.concatenate([wanted, filler], axis=1)
    rank_key = jnp.concatenate([status, jnp.ones((peer_count, slots), jnp.int32)], axis=1)
    picked = jnp.argsort(rank_key, axis=1, stable=True)[:, :slots]
    taken_ids = jnp.take_along_axis(source_pool, picked, axis=1)
    shuffle = jax.random.randint(key_parts[3], (peer_count, slots), 0, 1 << 16, dtype=jnp.int32) * slots + jnp.arange(slots, dtype=jnp.int32)
    taken_ids = jnp.take_along_axis(taken_ids, jnp.argsort(shuffle, axis=1), axis=1)
    own_ids = (receiver * LEAF_DEV + jnp.arange(LEAF_DEV, dtype=jnp.int32)[None, :])[..., None]
    near_lists = jnp.concatenate([own_ids, taken_ids.reshape(peer_count, LEAF_DEV, NEAR - 1)], axis=2)
    return near_lists.reshape(peer_count * LEAF_DEV, NEAR).astype(jnp.int32)


def far_partners(key, clusters):
    per_dev = clusters // PEERS
    entries = per_dev * FAR
    key_parts = jax.random.split(key, 3)
    column = jnp.arange(entries, dtype=jnp.int32)[None, :]
    offsets = jax.random.randint(key_parts[0], (PEERS, entries), 1, PEERS, dtype=jnp.int32)
    offsets = jnp.where(column < FARCAP, 1, offsets)
    pick = jax.random.randint(key_parts[1], (PEERS, entries), 0, FARCAP, dtype=jnp.int32)
    pick = jnp.where(column < FARCAP, column, pick)
    scores = jax.random.randint(key_parts[2], (PEERS, PEERS, per_dev), 0, 1 << 20, dtype=jnp.int32)
    scores = scores * per_dev + jnp.arange(per_dev, dtype=jnp.int32)
    candidates = jnp.argsort(scores, axis=-1).astype(jnp.int32)[..., :FARCAP]
    device = jnp.arange(PEERS, dtype=jnp.int32)[:, None]
    target = (device + offsets) % PEERS
    local = candidates[device, target, pick]
    return (target * per_dev + local).reshape(clusters, FAR).astype(jnp.int32)


def draw_near_source(key, part):
    key = jax.random.fold_in(key, 3)
    return near_plan(key)


def draw_far_one(key, part):
    key = jax.random.fold_in(key, 7)
    return far_partners(key, CL_ONE)


def draw_far_two(key, part):
    key = jax.random.fold_in(key, 11)
    return far_partners(key, CL_TWO)


def block_scale(stream_key, dims, pieces, least, largest):
    factor_of, own = 1.0, jax.random.fold_in(stream_key, 6)
    for axis_at, parts in pieces:
        draws = jnp.exp(jax.random.uniform(jax.random.fold_in(own, axis_at), (parts,), jnp.float32, least / len(pieces), largest / len(pieces)))
        factor_of = factor_of * jnp.repeat(draws, dims[axis_at] // parts).reshape([-1 if axis == axis_at else 1 for axis in range(len(dims))])
    return factor_of


def centred(stream_key, dims, spread, most, cuts=(), kind=jnp.bfloat16):
    drawn = jax.random.normal(stream_key, dims, jnp.float32) * spread
    if len(cuts) > 0:
        drawn = block_scale(stream_key, dims, cuts, -0.22, 0.18) * drawn
    return jnp.clip(drawn, min=-most, max=most).astype(kind)


def setup_inputs(seed: int = 0) -> dict:
    streams_of = jax.random.split(jax.random.key(seed), 11)
    return {
        "points": centred(streams_of[0], (DIM, POINTS), DIM ** -0.5, 1.0, ((1, 128),)),
        "rhs": centred(streams_of[1], (NRHS, POINTS), 1.0, 6.0, ((1, 128),)),
        "basis": centred(streams_of[2], (RANK, POINTS), LEAF ** -0.5, 0.375, ((1, 128),)),
        "transfer_one": centred(streams_of[3], (CL_ONE, RANK, 4 * RANK), RANK ** -0.5, 0.75, ((0, 128),)),
        "transfer_two": centred(streams_of[4], (CL_TWO, RANK, 4 * RANK), RANK ** -0.5, 0.75, ((0, 128),)),
        "skeleton_one": centred(streams_of[5], (DIM, CL_ONE * RANK), DIM ** -0.5, 1.0, ((1, 128),)),
        "skeleton_two": centred(streams_of[6], (DIM, CL_TWO * RANK), DIM ** -0.5, 1.0, ((1, 128),)),
        "near_source": draw_near_source(jax.random.fold_in(streams_of[10], 71), 0),
        "far_one": draw_far_one(jax.random.fold_in(streams_of[10], 71), 0),
        "far_two": draw_far_two(jax.random.fold_in(streams_of[10], 71), 0),
    }


kernel_scale = 2.0


def near_group(group_items, every_block):
    target_block, leaf_ids = group_items
    sources = every_block[leaf_ids]
    target_points = target_block[:, :DIM].astype(jnp.float32)
    source_points = sources[:, :, :DIM].astype(jnp.float32)
    target_sq = jnp.sum(target_points * target_points, axis=1)
    source_sq = jnp.sum(source_points * source_points, axis=2)
    inner_prod = jnp.einsum("gdp,gkdq->gkpq", target_points, source_points)
    distance = target_sq[:, None, :, None] + source_sq[:, :, None, :] - 2.0 * inner_prod
    weights = jnp.exp(-kernel_scale * distance).astype(jnp.bfloat16).astype(jnp.float32)
    return jnp.einsum("gkpq,gknq->gnp", weights, sources[:, :, DIM:].astype(jnp.float32))


def far_level(skeleton, coeffs, partners):
    clusters = partners.shape[0]
    skeleton_grid = skeleton.reshape(DIM, clusters, RANK).astype(jnp.float32)
    squares = jnp.sum(skeleton_grid * skeleton_grid, axis=0)
    picked = skeleton_grid[:, partners]
    inner_prod = jnp.einsum("dcr,dcfq->cfrq", skeleton_grid, picked)
    distance = squares[:, None, :, None] + squares[partners][:, :, None, :] - 2.0 * inner_prod
    weights = jnp.exp(-kernel_scale * distance).astype(jnp.bfloat16).astype(jnp.float32)
    return jnp.einsum("cfrq,cfnq->cnr", weights, coeffs[partners].astype(jnp.float32))


def lift(children, transfer):
    clusters = transfer.shape[0]
    joined = children.reshape(clusters, 4, NRHS, RANK).transpose(0, 2, 1, 3).reshape(clusters, NRHS, 4 * RANK)
    return jnp.einsum("cnk,crk->cnr", joined.astype(jnp.float32), transfer.astype(jnp.float32)).astype(jnp.bfloat16)


def lower(parents, transfer):
    clusters = transfer.shape[0]
    joined = jnp.einsum("cnr,crk->cnk", parents, transfer.astype(jnp.float32), precision=lax.Precision.HIGHEST)
    return joined.reshape(clusters, NRHS, 4, RANK).transpose(0, 2, 1, 3).reshape(4 * clusters, NRHS, RANK)


def reference(points, rhs, basis, transfer_one, transfer_two, skeleton_one, skeleton_two, near_source, far_one, far_two):
    row_width = DIM + NRHS
    every_block = jnp.concatenate([points.reshape(DIM, LEAVES, LEAF), rhs.reshape(NRHS, LEAVES, LEAF)], axis=0).transpose(1, 0, 2)

    def near_step(group_items):
        return near_group(group_items, every_block)

    near_part = lax.map(near_step, (every_block.reshape(LEAVES // 2, 2, row_width, LEAF), near_source.reshape(LEAVES // 2, 2, NEAR)))
    near_field = near_part.reshape(LEAVES, NRHS, LEAF).transpose(1, 0, 2)
    rhs_grid = rhs.reshape(NRHS, LEAVES, LEAF).astype(jnp.float32)
    basis_grid = basis.reshape(RANK, LEAVES, LEAF).astype(jnp.float32)
    leaf_coeff = jnp.einsum("nlp,rlp->lnr", rhs_grid, basis_grid).astype(jnp.bfloat16)
    coeff_one = lift(leaf_coeff, transfer_one)
    coeff_two = lift(coeff_one, transfer_two)
    field_two = far_level(skeleton_two, coeff_two, far_two)
    field_one = far_level(skeleton_one, coeff_one, far_one)
    down_one = field_one + lower(field_two, transfer_two)
    down_leaf = lower(down_one, transfer_one).astype(jnp.bfloat16)
    far_out = jnp.einsum("lnr,rlp->nlp", down_leaf.astype(jnp.float32), basis_grid)
    return (near_field + far_out).reshape(NRHS, POINTS).astype(jnp.bfloat16)
```

```python
import jax
import jax.numpy as jnp
from jax import lax
from jax.experimental import pallas as pl
from jax.experimental.pallas import tpu as pltpu
from jax.sharding import PartitionSpec as P

DIM = 32
NRHS = 16
RANK = 64
LEAF = 256
NEAR = 10
FAR = 8
LEAVES = 32
ONE = 8
TWO = 2
PAIRS = ONE // 2 + TWO // 2
ROWS = DIM + NRHS
PEERS = 128
LOCAL = 2 * PEERS + 4
TABLE = LOCAL + LEAVES
LOG2E = 1.4426950408889634
MIB = 1 << 20

NT = (((1,), (1,)), ((), ()))
NN = (((1,), (0,)), ((), ()))


def dot(a, b, dims=NN):
    return lax.dot_general(a, b, dims, preferred_element_type=jnp.float32)


def vmem(limit=48):
    return pltpu.CompilerParams(vmem_limit_bytes=limit * MIB)


ANY = pl.BlockSpec(memory_space=pl.ANY)
VM = pl.BlockSpec(memory_space=pltpu.VMEM)
SM = pl.BlockSpec(memory_space=pltpu.SMEM)


def pack_kernel(
    source_ref, points_ref, rhs_ref, msg_ref, right_ref, left_ref, block_ref,
    row_ref, row_smem, row_sem, msg_sem, side_sem,
):
    me = lax.axis_index("leaf")
    for leaf in range(LEAVES):
        columns = pl.ds(leaf * LEAF, LEAF)
        block_ref[leaf, :DIM, :] = points_ref[:, columns]
        block_ref[leaf, DIM:, :] = rhs_ref[:, columns]
    width = PEERS * LEAVES
    low = high = bits = None
    for k in range(NEAR):
        mine = source_ref[k : k + 1, :] - me * LEAVES
        inside = (mine >> 5) == 0
        a = jnp.where(inside, mine, LEAVES)
        b = jnp.where(inside, mine, -1)
        c = jnp.where(inside, 1 << (mine & 31), 0)
        low = a if k == 0 else jnp.minimum(low, a)
        high = b if k == 0 else jnp.maximum(high, b)
        bits = c if k == 0 else bits | c
    low, high, bits = (jnp.broadcast_to(v, (8, width)) for v in (low, high, bits))
    for step in (16, 8, 4, 2, 1):
        low = jnp.minimum(low, pltpu.roll(low, width - step, 1))
        high = jnp.maximum(high, pltpu.roll(high, width - step, 1))
        bits = bits | pltpu.roll(bits, width - step, 1)
    place = lax.broadcasted_iota(jnp.int32, (8, width), 1) & 31
    row_ref[...] = jnp.where(
        place == 0, low, jnp.where(place == 1, pltpu.roll(high, 1, 1), pltpu.roll(bits, 2, 1))
    )
    copy = pltpu.make_async_copy(row_ref.at[0:1], row_smem, row_sem)
    copy.start()
    copy.wait()

    def send(peer, _):
        for slot in range(2):
            leaf = row_smem[0, peer * LEAVES + slot] & 31
            pltpu.make_async_copy(block_ref.at[leaf], msg_ref.at[peer, slot], msg_sem).start()
        return 0

    lax.fori_loop(0, PEERS, send, 0, unroll=4)
    for side, (ref, step) in enumerate(((right_ref, 1), (left_ref, PEERS - 1))):
        at = lax.rem(me + step, PEERS) * LEAVES
        between = row_smem[0, at + 2]
        between = between & ~(1 << (row_smem[0, at] & 31)) & ~(1 << (row_smem[0, at + 1] & 31))

        def scan(bit, found):
            has = ((between >> bit) & 1) == 1
            return jnp.where(has & (found[0] < 0), bit, found[0]), jnp.where(has, bit, found[1])

        first, last = lax.fori_loop(0, LEAVES, scan, (jnp.int32(-1), jnp.int32(0)))
        for slot, leaf in enumerate((first & 31, last & 31)):
            pltpu.make_async_copy(block_ref.at[leaf], ref.at[slot], side_sem.at[side]).start()
    pltpu.make_async_copy(msg_ref, msg_ref, msg_sem).wait()
    for side, ref in enumerate((right_ref, left_ref)):
        pltpu.make_async_copy(ref, ref, side_sem.at[side]).wait()


def pack(source, points, rhs):
    block = jax.ShapeDtypeStruct((LEAVES, ROWS, LEAF), jnp.bfloat16)
    side = jax.ShapeDtypeStruct((2, ROWS, LEAF), jnp.bfloat16)
    return pl.pallas_call(
        pack_kernel,
        out_shape=(
            jax.ShapeDtypeStruct((PEERS, 2, ROWS, LEAF), jnp.bfloat16), side, side, block,
        ),
        in_specs=[VM, VM, VM],
        out_specs=(ANY, ANY, ANY, VM),
        scratch_shapes=[
            pltpu.VMEM((8, PEERS * LEAVES), jnp.int32),
            pltpu.SMEM((1, PEERS * LEAVES), jnp.int32),
            pltpu.SemaphoreType.DMA,
            pltpu.SemaphoreType.DMA,
            pltpu.SemaphoreType.DMA((2,)),
        ],
        compiler_params=vmem(),
        name="pack",
    )(source.T, points, rhs)


def upper(b):
    return jnp.concatenate([b, jnp.zeros_like(b)], axis=0)


def below(b):
    return jnp.concatenate([jnp.zeros_like(b), b], axis=0)


def coeff_kernel(rhs_ref, basis_ref, one_ref, two_ref, skel_one_ref, skel_two_ref, out_ref):
    def leaf_pair(leaf):
        a, b = (pl.ds((leaf + i) * LEAF, LEAF) for i in range(2))
        return (
            dot(rhs_ref[:, a], upper(basis_ref[:, a]), NT)
            + dot(rhs_ref[:, b], below(basis_ref[:, b]), NT)
        ).astype(jnp.bfloat16)

    def lift_pair(children, transfer_ref, cluster):
        return (
            dot(children[0], upper(transfer_ref[cluster]), NT)
            + dot(children[1], below(transfer_ref[cluster + 1]), NT)
        ).astype(jnp.bfloat16)

    pairs = []
    for pair in range(ONE // 2):
        joined = [
            jnp.concatenate([leaf_pair(4 * c), leaf_pair(4 * c + 2)], axis=1)
            for c in (2 * pair, 2 * pair + 1)
        ]
        pairs.append(lift_pair(joined, one_ref, 2 * pair))
        out_ref[pair, :DIM, :] = skel_one_ref[:, pl.ds(pair * 2 * RANK, 2 * RANK)]
        out_ref[pair, DIM:, :] = pairs[-1]
    joined = [jnp.concatenate(pairs[2 * e : 2 * e + 2], axis=1) for e in range(TWO)]
    out_ref[PAIRS - 1, :DIM, :] = skel_two_ref[...]
    out_ref[PAIRS - 1, DIM:, :] = lift_pair(joined, two_ref, 0)


def coefficients(rhs, basis, transfer_one, transfer_two, skeleton_one, skeleton_two):
    return pl.pallas_call(
        coeff_kernel,
        out_shape=jax.ShapeDtypeStruct((PAIRS, ROWS, 2 * RANK), jnp.bfloat16),
        in_specs=[VM] * 6,
        out_specs=VM,
        compiler_params=vmem(),
        name="coefficients",
    )(rhs, basis, transfer_one, transfer_two, skeleton_one, skeleton_two)


def table_rows(near_source, me):
    mine = lax.dynamic_slice_in_dim(near_source, me * LEAVES, LEAVES, 0).reshape(-1)
    device, leaf = mine >> 5, mine & 31
    from_peer = device[:, None] == jnp.arange(PEERS, dtype=jnp.int32)[None, :]
    low = jnp.min(jnp.where(from_peer, leaf[:, None], LEAVES), axis=0)
    high = jnp.max(jnp.where(from_peer, leaf[:, None], -1), axis=0)
    low_of = jnp.sum(jnp.where(from_peer, low[None, :], 0), axis=1)
    high_of = jnp.sum(jnp.where(from_peer, high[None, :], 0), axis=1)
    row = 2 * device + (leaf != low_of)
    inner = (leaf > low_of) & (leaf < high_of)
    for side, step in enumerate((PEERS - 1, 1)):
        chosen = inner & (device == (me + step) % PEERS)
        first = jnp.min(jnp.where(chosen, leaf, LEAVES))
        row = jnp.where(chosen, 2 * PEERS + 2 * side + (leaf != first), row)
    return jnp.where(device == me, LOCAL + leaf, row)


def near_kernel(
    row_ref, arrived_ref, left_ref, right_ref, own_ref, out_ref, table_ref, sem
):
    copies = [
        pltpu.make_async_copy(ref, table_ref.at[pl.ds(at, ref.shape[0])], sem.at[i])
        for i, (ref, at) in enumerate(
            ((arrived_ref, 0), (left_ref, 2 * PEERS), (right_ref, 2 * PEERS + 2), (own_ref, LOCAL))
        )
    ]
    for copy in copies:
        copy.start()
    for copy in copies:
        copy.wait()

    def step(leaf, _):
        target = table_ref[LOCAL + leaf, :DIM, :].astype(jnp.float32).T
        target_sq = jnp.sum(target * target, axis=1, keepdims=True) * (2 * LOG2E)
        target = target.astype(jnp.bfloat16)
        total = jnp.zeros((NRHS, LEAF), jnp.float32)
        for k in range(NEAR):
            row = row_ref[leaf * NEAR + k]
            source = table_ref[row, :DIM, :]
            wide = source.astype(jnp.float32)
            source_sq = jnp.sum(wide * wide, axis=0, keepdims=True) * (2 * LOG2E)
            power = dot(target, source) * (4 * LOG2E) - target_sq - source_sq
            weights = jnp.exp2(power).astype(jnp.bfloat16)
            total += dot(table_ref[row, DIM:, :], weights, NT)
        out_ref[:, pl.ds(pl.multiple_of(leaf * LEAF, LEAF), LEAF)] = total
        return 0

    lax.fori_loop(0, LEAVES, step, 0)


def near_field(rows, arrived, left, right, own):
    return pl.pallas_call(
        near_kernel,
        out_shape=jax.ShapeDtypeStruct((NRHS, LEAVES * LEAF), jnp.float32),
        in_specs=[SM, ANY, ANY, ANY, ANY],
        out_specs=VM,
        scratch_shapes=[
            pltpu.VMEM((TABLE, ROWS, LEAF), jnp.bfloat16),
            pltpu.SemaphoreType.DMA((4,)),
        ],
        compiler_params=vmem(),
        cost_estimate=pl.CostEstimate(
            flops=2 * 320 * 65536 * 48, bytes_accessed=8 * MIB, transcendentals=320 * 65536
        ),
        name="near_field",
    )(rows, arrived, left, right, own)


def far_kernel(
    far_one_ref, far_two_ref, gathered_ref, skel_one_ref, skel_two_ref, one_ref, two_ref,
    basis_ref, near_ref, out_ref, picked_ref, sem,
):
    for c in range(ONE):
        for j in range(FAR):
            b = far_one_ref[c, j]
            pltpu.make_async_copy(
                gathered_ref.at[(b >> 3) * PAIRS + ((b & 7) >> 1)], picked_ref.at[c * FAR + j], sem
            ).start()
    for e in range(TWO):
        for j in range(FAR):
            b = far_two_ref[e, j]
            pltpu.make_async_copy(
                gathered_ref.at[(b >> 1) * PAIRS + PAIRS - 1],
                picked_ref.at[(ONE + e) * FAR + j],
                sem,
            ).start()
    pltpu.make_async_copy(picked_ref, picked_ref, sem).wait()
    half_of = lax.broadcasted_iota(jnp.int32, (NRHS, 2 * RANK), 1) >> 6

    def split(x):
        high = x.astype(jnp.bfloat16)
        return jnp.concatenate([high, (x - high.astype(jnp.float32)).astype(jnp.bfloat16)], axis=0)

    def exact(parts, b):
        both = dot(parts, b)
        return both[:NRHS] + both[NRHS:]

    def turned(skel_ref, pair):
        return skel_ref[:, pl.ds(pair * 2 * RANK, 2 * RANK)].astype(jnp.float32).T

    def field_pair(skel_ref, partners_ref, pair, at):
        both = turned(skel_ref, pair)
        total = None
        for i, padded in enumerate((upper, below)):
            c = 2 * pair + i
            target = both[i * RANK : (i + 1) * RANK]
            target_sq = jnp.sum(target * target, axis=1, keepdims=True) * (2 * LOG2E)
            blocks = [picked_ref[(at + c) * FAR + j] for j in range(FAR)]
            source = jnp.concatenate([block[:DIM] for block in blocks], axis=1)
            coeffs = jnp.concatenate(
                [
                    jnp.where(half_of == (partners_ref[c, j] & 1), blocks[j][DIM:], 0)
                    for j in range(FAR)
                ],
                axis=1,
            )
            wide = source.astype(jnp.float32)
            source_sq = jnp.sum(wide * wide, axis=0, keepdims=True) * (2 * LOG2E)
            power = dot(target.astype(jnp.bfloat16), source) * (4 * LOG2E) - target_sq - source_sq
            weights = jnp.exp2(power).astype(jnp.bfloat16)
            term = dot(coeffs, padded(weights), NT)
            total = term if i == 0 else total + term
        return total

    field_two = split(field_pair(skel_two_ref, far_two_ref, 0, ONE))
    from_two = [
        exact(field_two, padded(two_ref[e])) for e, padded in enumerate((upper, below))
    ]
    for pair in range(ONE // 2):
        parent = from_two[pair // 2][:, (pair % 2) * 2 * RANK : (pair % 2 + 1) * 2 * RANK]
        down_one = split(field_pair(skel_one_ref, far_one_ref, pair, 0) + parent)
        for i, padded in enumerate((upper, below)):
            c = 2 * pair + i
            down_leaf = exact(down_one, padded(one_ref[c])).astype(jnp.bfloat16)
            for leaf in range(4):
                columns = pl.ds((4 * c + leaf) * LEAF, LEAF)
                half = down_leaf[:, (leaf // 2) * 2 * RANK : (leaf // 2 + 1) * 2 * RANK]
                basis = (upper, below)[leaf % 2](basis_ref[:, columns])
                out_ref[:, columns] = (near_ref[:, columns] + dot(half, basis)).astype(
                    jnp.bfloat16
                )


def far_field(far_one, far_two, gathered, skeleton_one, skeleton_two, transfer_one, transfer_two,
              basis, near):
    return pl.pallas_call(
        far_kernel,
        out_shape=jax.ShapeDtypeStruct((NRHS, LEAVES * LEAF), jnp.bfloat16),
        in_specs=[SM, SM, ANY] + [VM] * 6,
        out_specs=VM,
        scratch_shapes=[
            pltpu.VMEM(((ONE + TWO) * FAR, ROWS, 2 * RANK), jnp.bfloat16),
            pltpu.SemaphoreType.DMA,
        ],
        compiler_params=vmem(),
        name="far_field",
    )(far_one, far_two, gathered, skeleton_one, skeleton_two, transfer_one, transfer_two, basis,
      near)


def shift(x, step):
    return lax.ppermute(x, "leaf", [(i, (i + step) % PEERS) for i in range(PEERS)])


def local(
    points, rhs, basis, transfer_one, transfer_two, skeleton_one, skeleton_two, near_source,
    far_one, far_two,
):
    me = lax.axis_index("leaf")
    message, to_right, to_left, own = pack(near_source, points, rhs)
    columns = coefficients(rhs, basis, transfer_one, transfer_two, skeleton_one, skeleton_two)
    gathered = lax.all_gather(columns, "leaf", axis=0, tiled=True)
    arrived = lax.all_to_all(message, "leaf", split_axis=0, concat_axis=0, tiled=True)
    from_left, from_right = shift(to_right, 1), shift(to_left, -1)
    rows = table_rows(near_source, me)
    near = near_field(
        rows, arrived.reshape(2 * PEERS, ROWS, LEAF), from_left, from_right, own
    )
    return far_field(far_one, far_two, gathered, skeleton_one, skeleton_two, transfer_one,
                     transfer_two, basis, near)


def solution(mesh):
    placed = (
        P(None, "leaf"),
        P(None, "leaf"),
        P(None, "leaf"),
        P("leaf", None, None),
        P("leaf", None, None),
        P(None, "leaf"),
        P(None, "leaf"),
        P(),
        P("leaf", None),
        P("leaf", None),
    )
    return jax.shard_map(
        local, mesh=mesh, in_specs=placed, out_specs=P(None, "leaf"), check_vma=False
    )
```

```python
import jax
import jax.numpy as jnp
from jax import lax
from jax.experimental import pallas as pl
from jax.experimental.pallas import tpu as pltpu
from jax.sharding import PartitionSpec as P

DIM = 32
NRHS = 16
RANK = 64
LEAF = 256
NEAR = 10
FAR = 8
LEAVES = 32
ONE = 8
TWO = 2
PAIRS = ONE // 2
ROWS = DIM + NRHS
PEERS = 128
LOCAL = 2 * PEERS + 4
TABLE = LOCAL + LEAVES
GROUP = 16
LIST = 384
STRIDE = 512
HALF_ROWS = ROWS // 2
MESSAGE = ROWS + HALF_ROWS
MIB = 1 << 20

NT = (((1,), (1,)), ((), ()))
NN = (((1,), (0,)), ((), ()))


def dot(a, b, dims=NN):
    return lax.dot_general(a, b, dims, preferred_element_type=jnp.float32)


def vmem(limit=56):
    return pltpu.CompilerParams(vmem_limit_bytes=limit * MIB)


def cost(flops, moved, exps=0):
    return pl.CostEstimate(flops=flops, bytes_accessed=moved, transcendentals=exps)


def fetch(sem, *pairs):
    copies = [pltpu.make_async_copy(a, b, sem.at[i]) for i, (a, b) in enumerate(pairs)]
    for copy in copies:
        copy.start()
    return copies


def bf16(*shape):
    return pltpu.VMEM(shape, jnp.bfloat16)


ANY = pl.BlockSpec(memory_space=pl.ANY)
VM = pl.BlockSpec(memory_space=pltpu.VMEM)
SM = pl.BlockSpec(memory_space=pltpu.SMEM)


def ask_kernel(far_ref, ask_ref, low_ref):
    peer = lax.broadcasted_iota(jnp.int32, (PEERS, FAR), 0) * ONE
    low = high = None
    for i in range(ONE):
        at = far_ref[i : i + 1, :] - peer
        inside = (at >> 3) == 0
        a, b = jnp.where(inside, at, ONE), jnp.where(inside, at, -1)
        low = a if i == 0 else jnp.minimum(low, a)
        high = b if i == 0 else jnp.maximum(high, b)
    low = jnp.min(low.astype(jnp.float32), axis=1, keepdims=True)
    high = jnp.max(high.astype(jnp.float32), axis=1, keepdims=True)
    lane = lax.broadcasted_iota(jnp.int32, (PEERS, PEERS), 1)
    ask_ref[...] = jnp.where(lane == 0, low, high).astype(jnp.int32)
    across = lax.broadcasted_iota(jnp.int32, (ONE, PEERS), 1) * ONE
    low = None
    for j in range(FAR):
        at = far_ref[:, j : j + 1] - across
        a = jnp.where((at >> 3) == 0, at, ONE)
        low = a if j == 0 else jnp.minimum(low, a)
    low = jnp.min(low.astype(jnp.float32), axis=0, keepdims=True)
    low_ref[...] = jnp.broadcast_to(low, (ONE, PEERS)).astype(jnp.int32)


def ask(far_one):
    return pl.pallas_call(
        ask_kernel,
        out_shape=(
            jax.ShapeDtypeStruct((PEERS, PEERS), jnp.int32),
            jax.ShapeDtypeStruct((ONE, PEERS), jnp.int32),
        ),
        in_specs=[VM],
        out_specs=(VM, VM),
        compiler_params=vmem(),
        name="ask",
    )(far_one)


def pack_kernel(
    source_ref, points_ref, rhs_ref, msg_ref, right_ref, left_ref, own_ref,
    lists_ref, block_ref, row_ref, row_smem, in_sem, row_sem, msg_sem, side_sem,
):
    me = lax.axis_index("leaf")
    listed = pltpu.make_async_copy(source_ref, lists_ref, row_sem)
    listed.start()
    filled = fetch(
        in_sem,
        *(
            (ref.at[:, pl.ds(leaf * LEAF, LEAF)], block_ref.at[leaf, rows])
            for leaf in range(LEAVES)
            for ref, rows in ((points_ref, pl.ds(0, DIM)), (rhs_ref, pl.ds(DIM, NRHS)))
        ),
    )
    listed.wait()
    width = PEERS * LEAVES
    low = high = bits = None
    for k in range(NEAR):
        mine = lists_ref[k : k + 1, :] - me * LEAVES
        inside = (mine >> 5) == 0
        a = jnp.where(inside, mine, LEAVES)
        b = jnp.where(inside, mine, -1)
        c = jnp.where(inside, 1 << (mine & 31), 0)
        low = a if k == 0 else jnp.minimum(low, a)
        high = b if k == 0 else jnp.maximum(high, b)
        bits = c if k == 0 else bits | c
    low, high, bits = (jnp.broadcast_to(v, (8, width)) for v in (low, high, bits))
    for step in (16, 8, 4, 2, 1):
        low = jnp.minimum(low, pltpu.roll(low, width - step, 1))
        high = jnp.maximum(high, pltpu.roll(high, width - step, 1))
        bits = bits | pltpu.roll(bits, width - step, 1)
    place = lax.broadcasted_iota(jnp.int32, (8, width), 1) & 31
    row_ref[...] = jnp.where(
        place == 0, low, jnp.where(place == 1, pltpu.roll(high, 1, 1), pltpu.roll(bits, 2, 1))
    )
    copy = pltpu.make_async_copy(row_ref.at[0:1], row_smem, row_sem)
    copy.start()
    for fill in filled:
        fill.wait()
    own = pltpu.make_async_copy(block_ref, own_ref, in_sem.at[0])
    own.start()
    copy.wait()

    def send(peer, _):
        for slot in range(2):
            leaf = row_smem[0, peer * LEAVES + slot] & 31
            pltpu.make_async_copy(block_ref.at[leaf], msg_ref.at[peer, slot], msg_sem).start()
        return 0

    lax.fori_loop(0, PEERS, send, 0, unroll=4)
    for side, (ref, step) in enumerate(((right_ref, 1), (left_ref, PEERS - 1))):
        at = lax.rem(me + step, PEERS) * LEAVES
        between = row_smem[0, at + 2]
        between = between & ~(1 << (row_smem[0, at] & 31)) & ~(1 << (row_smem[0, at + 1] & 31))

        def scan(bit, found):
            has = ((between >> bit) & 1) == 1
            return jnp.where(has & (found[0] < 0), bit, found[0]), jnp.where(has, bit, found[1])

        first, last = lax.fori_loop(0, LEAVES, scan, (jnp.int32(-1), jnp.int32(0)))
        for slot, leaf in enumerate((first & 31, last & 31)):
            pltpu.make_async_copy(block_ref.at[leaf], ref.at[slot], side_sem.at[side]).start()
    pltpu.make_async_copy(msg_ref, msg_ref, msg_sem).wait()
    for side, ref in enumerate((right_ref, left_ref)):
        pltpu.make_async_copy(ref, ref, side_sem.at[side]).wait()
    own.wait()


def pack(source, points, rhs):
    block = jax.ShapeDtypeStruct((LEAVES, ROWS, LEAF), jnp.bfloat16)
    side = jax.ShapeDtypeStruct((2, ROWS, LEAF), jnp.bfloat16)
    return pl.pallas_call(
        pack_kernel,
        out_shape=(
            jax.ShapeDtypeStruct((PEERS, 2, ROWS, LEAF), jnp.bfloat16), side, side, block,
        ),
        in_specs=[ANY, ANY, ANY],
        out_specs=(ANY, ANY, ANY, ANY),
        scratch_shapes=[
            pltpu.VMEM((NEAR, PEERS * LEAVES), jnp.int32),
            bf16(LEAVES, ROWS, LEAF),
            pltpu.VMEM((8, PEERS * LEAVES), jnp.int32),
            pltpu.SMEM((1, PEERS * LEAVES), jnp.int32),
            pltpu.SemaphoreType.DMA((2 * LEAVES,)),
            pltpu.SemaphoreType.DMA,
            pltpu.SemaphoreType.DMA,
            pltpu.SemaphoreType.DMA((2,)),
        ],
        compiler_params=vmem(),
        cost_estimate=cost(1 << 20, 14 * MIB),
        name="pack",
    )(source.T, points, rhs)


def upper(b):
    return jnp.concatenate([b, jnp.zeros_like(b)], axis=0)


def below(b):
    return jnp.concatenate([jnp.zeros_like(b), b], axis=0)


def coeff_kernel(
    rhs_hbm, basis_hbm, one_hbm, two_hbm, skel_one_hbm, skel_two_hbm, out_ref,
    rhs_ref, basis_ref, one_ref, two_ref, skel_one_ref, skel_two_ref, sem,
):
    for copy in fetch(
        sem, (rhs_hbm, rhs_ref), (basis_hbm, basis_ref), (one_hbm, one_ref), (two_hbm, two_ref),
        (skel_one_hbm, skel_one_ref), (skel_two_hbm, skel_two_ref),
    ):
        copy.wait()

    def leaf_pair(leaf):
        a, b = (pl.ds((leaf + i) * LEAF, LEAF) for i in range(2))
        return (
            dot(rhs_ref[:, a], upper(basis_ref[:, a]), NT)
            + dot(rhs_ref[:, b], below(basis_ref[:, b]), NT)
        ).astype(jnp.bfloat16)

    def lift_pair(children, transfer_ref, cluster):
        return (
            dot(children[0], upper(transfer_ref[cluster]), NT)
            + dot(children[1], below(transfer_ref[cluster + 1]), NT)
        ).astype(jnp.bfloat16)

    pairs = []
    for pair in range(PAIRS):
        joined = [
            jnp.concatenate([leaf_pair(4 * c), leaf_pair(4 * c + 2)], axis=1)
            for c in (2 * pair, 2 * pair + 1)
        ]
        pairs.append(lift_pair(joined, one_ref, 2 * pair))
        out_ref[pair, :DIM, :] = skel_one_ref[:, pl.ds(pair * 2 * RANK, 2 * RANK)]
        out_ref[pair, DIM:, :] = pairs[-1]
    joined = [jnp.concatenate(pairs[2 * e : 2 * e + 2], axis=1) for e in range(TWO)]
    out_ref[PAIRS, :DIM, :] = skel_two_ref[...]
    out_ref[PAIRS, DIM:, :] = lift_pair(joined, two_ref, 0)


def coefficients(*args):
    return pl.pallas_call(
        coeff_kernel,
        out_shape=jax.ShapeDtypeStruct((PAIRS + 1, ROWS, 2 * RANK), jnp.bfloat16),
        in_specs=[ANY] * 6,
        out_specs=VM,
        scratch_shapes=[bf16(*a.shape) for a in args] + [pltpu.SemaphoreType.DMA((6,))],
        compiler_params=vmem(),
        cost_estimate=cost(1 << 26, 2 * MIB),
        name="coefficients",
    )(*args)


def far_pack_kernel(asked_ref, columns_ref, out_ref, low_ref, high_ref):
    left = lax.broadcasted_iota(jnp.int32, (ROWS, 2 * RANK), 1) < RANK
    for pair in range(PAIRS):
        wide = columns_ref[pair].astype(jnp.float32)
        turned = pltpu.roll(wide, RANK, 1)
        low_ref[2 * pair] = high_ref[2 * pair + 1] = wide
        low_ref[2 * pair + 1] = high_ref[2 * pair] = turned
    wide = columns_ref[PAIRS].astype(jnp.float32)
    turned = pltpu.roll(wide, RANK, 1)
    half = left[:HALF_ROWS]
    second = (
        jnp.where(half, wide[:HALF_ROWS], turned[HALF_ROWS:]),
        jnp.where(half, turned[:HALF_ROWS], wide[HALF_ROWS:]),
    )

    def fill(chip, _):
        for core in range(2):
            peer = 2 * chip + core
            first = jnp.where(
                left, low_ref[asked_ref[2 * peer] & 7], high_ref[asked_ref[2 * peer + 1] & 7]
            )
            out_ref[peer] = jnp.concatenate([first, second[core]], axis=0).astype(jnp.bfloat16)
        return 0

    lax.fori_loop(0, PEERS // 2, fill, 0, unroll=2)


def far_pack(asked, columns):
    return pl.pallas_call(
        far_pack_kernel,
        out_shape=jax.ShapeDtypeStruct((PEERS, MESSAGE, 2 * RANK), jnp.bfloat16),
        in_specs=[SM, VM],
        out_specs=VM,
        scratch_shapes=[pltpu.VMEM((ONE, ROWS, 2 * RANK), jnp.float32)] * 2,
        compiler_params=vmem(),
        cost_estimate=cost(1 << 20, 5 * MIB),
        name="far_pack",
    )(asked, columns)


def table_rows(near_source, me):
    mine = lax.dynamic_slice_in_dim(near_source, me * LEAVES, LEAVES, 0).reshape(-1)
    device, leaf = mine >> 5, mine & 31
    from_peer = device[:, None] == jnp.arange(PEERS, dtype=jnp.int32)[None, :]
    low = jnp.min(jnp.where(from_peer, leaf[:, None], LEAVES), axis=0)
    high = jnp.max(jnp.where(from_peer, leaf[:, None], -1), axis=0)
    low_of = jnp.sum(jnp.where(from_peer, low[None, :], 0), axis=1)
    high_of = jnp.sum(jnp.where(from_peer, high[None, :], 0), axis=1)
    row = 2 * device + (leaf != low_of)
    inner = (leaf > low_of) & (leaf < high_of)
    for side, step in enumerate((PEERS - 1, 1)):
        chosen = inner & (device == (me + step) % PEERS)
        first = jnp.min(jnp.where(chosen, leaf, LEAVES))
        row = jnp.where(chosen, 2 * PEERS + 2 * side + (leaf != first), row)
    return jnp.where(device == me, LOCAL + leaf, row)


def with_square(block, first):
    wide = block.astype(jnp.float32)
    square = jnp.sum(wide * wide, axis=0, keepdims=True) * -2
    high = square.astype(jnp.bfloat16).astype(jnp.float32)
    middle = (square - high).astype(jnp.bfloat16).astype(jnp.float32)
    low = square - high - middle
    at = lax.broadcasted_iota(jnp.int32, (16, LEAF), 0)
    ones, parts = (3, 0) if first else (0, 3)
    extra = jnp.where((at >= ones) & (at < ones + 3), 1.0, 0.0)
    for i, part in enumerate((high, middle, low)):
        extra = jnp.where(at == parts + i, part, extra)
    if first:
        return jnp.concatenate([wide * 4, extra], axis=0).T.astype(jnp.bfloat16)
    return jnp.concatenate([block, extra.astype(jnp.bfloat16)], axis=0)


def turn_targets(own_ref, target_ref):
    def turn(leaf, _):
        target_ref[leaf, :, :ROWS] = with_square(own_ref[leaf, :DIM, :], True)
        return 0

    lax.fori_loop(0, LEAVES, turn, 0, unroll=2)


def add_pairs(list_ref, start, table_ref, target_ref, out_ref):
    def step(i, _):
        terms = []
        for u in range(GROUP):
            pair = list_ref[start + i * GROUP + u]
            target, row = pair // STRIDE, pair & (STRIDE - 1)
            weights = jnp.exp(
                dot(target_ref[target, :, :ROWS], with_square(table_ref[row, :DIM, :], False))
            ).astype(jnp.bfloat16)
            terms.append((target, dot(table_ref[row, DIM:, :], weights, NT)))
        for target, term in terms:
            columns = pl.ds(pl.multiple_of(target * LEAF, LEAF), LEAF)
            out_ref[:, columns] += term
        return 0

    lax.fori_loop(0, (list_ref[start + LIST - 1] + GROUP - 1) // GROUP, step, 0)


def own_kernel(row_ref, own_hbm, out_ref, list_ref, own_ref, target_ref, sem):
    (copy,) = fetch(sem, (own_hbm, own_ref.at[pl.ds(0, LEAVES)]))

    def sort(target, counts):
        mine, others = counts
        for k in range(NEAR):
            row = row_ref[target * NEAR + k]
            list_ref[mine] = target * STRIDE + jnp.maximum(row - LOCAL, 0)
            list_ref[LIST + others] = target * STRIDE + row
            is_mine = (row >= LOCAL).astype(jnp.int32)
            mine, others = mine + is_mine, others + 1 - is_mine
        return mine, others

    mine, others = lax.fori_loop(0, LEAVES, sort, (jnp.int32(0), jnp.int32(0)))
    for u in range(GROUP):
        list_ref[mine + u] = LEAVES
        list_ref[LIST + others + u] = LOCAL
    list_ref[LIST - 1] = mine
    list_ref[2 * LIST - 1] = others
    own_ref[LEAVES] = jnp.zeros((ROWS, LEAF), jnp.bfloat16)
    copy.wait()
    turn_targets(own_ref, target_ref)
    out_ref[...] = jnp.zeros_like(out_ref)
    add_pairs(list_ref, 0, own_ref, target_ref, out_ref)


def own_pairs(rows, own):
    return pl.pallas_call(
        own_kernel,
        out_shape=(
            jax.ShapeDtypeStruct((NRHS, LEAVES * LEAF), jnp.float32),
            jax.ShapeDtypeStruct((2 * LIST,), jnp.int32),
        ),
        in_specs=[SM, ANY],
        out_specs=(VM, SM),
        scratch_shapes=[
            bf16(LEAVES + 1, ROWS, LEAF),
            bf16(LEAVES, LEAF, 128),
            pltpu.SemaphoreType.DMA((1,)),
        ],
        compiler_params=vmem(),
        cost_estimate=cost(2 * 120 * 65536 * 272, 2 * MIB, 120 * 65536),
        name="own_pairs",
    )(rows, own)


def remote_kernel(
    list_ref, arrived_ref, left_ref, right_ref, own_hbm, field_ref, out_ref,
    table_ref, own_ref, target_ref, sem,
):
    near = fetch(
        sem,
        (own_hbm, own_ref),
        (field_ref, out_ref),
        (arrived_ref, table_ref.at[pl.ds(0, 2 * PEERS)]),
        (left_ref, table_ref.at[pl.ds(2 * PEERS, 2)]),
        (right_ref, table_ref.at[pl.ds(2 * PEERS + 2, 2)]),
    )
    table_ref[LOCAL] = jnp.zeros((ROWS, LEAF), jnp.bfloat16)
    near[0].wait()
    turn_targets(own_ref, target_ref)
    for copy in near[1:]:
        copy.wait()
    add_pairs(list_ref, LIST, table_ref, target_ref, out_ref)


def remote_pairs(lists, arrived, left, right, own, field):
    return pl.pallas_call(
        remote_kernel,
        out_shape=jax.ShapeDtypeStruct((NRHS, LEAVES * LEAF), jnp.float32),
        in_specs=[SM, ANY, ANY, ANY, ANY, ANY],
        out_specs=VM,
        scratch_shapes=[
            bf16(LOCAL + 1, ROWS, LEAF),
            bf16(LEAVES, ROWS, LEAF),
            bf16(LEAVES, LEAF, 128),
            pltpu.SemaphoreType.DMA((5,)),
        ],
        compiler_params=vmem(),
        cost_estimate=cost(2 * 200 * 65536 * 272, 8 * MIB, 200 * 65536),
        name="remote_pairs",
    )(lists, arrived, left, right, own, field)


def turned(skel_ref, pair):
    return skel_ref[:, pl.ds(pair * 2 * RANK, 2 * RANK)].astype(jnp.float32).T


def field_pair(targets, blocks, halves):
    half_of = lax.broadcasted_iota(jnp.int32, (NRHS, 2 * RANK), 1) >> 6
    total = None
    for i, padded in enumerate((upper, below)):
        target = targets[i * RANK : (i + 1) * RANK]
        target_sq = jnp.sum(target * target, axis=1, keepdims=True) * 2
        source = jnp.concatenate([block[:DIM] for block in blocks[i]], axis=1)
        coeffs = jnp.concatenate(
            [
                jnp.where(half_of == half, block[DIM:], 0)
                for block, half in zip(blocks[i], halves[i], strict=True)
            ],
            axis=1,
        )
        wide = source.astype(jnp.float32)
        source_sq = jnp.sum(wide * wide, axis=0, keepdims=True) * 2
        power = dot((target * 4).astype(jnp.bfloat16), source) - target_sq - source_sq
        weights = jnp.exp(power).astype(jnp.bfloat16)
        term = dot(coeffs, padded(weights), NT)
        total = term if i == 0 else total + term
    return total


def far_one_kernel(far_ref, low_ref, arrived_ref, skel_hbm, out_ref, skel_ref, picked_ref, sem, in_sem):
    (copy,) = fetch(in_sem, (skel_hbm, skel_ref))
    for c in range(ONE):
        for j in range(FAR):
            pltpu.make_async_copy(
                arrived_ref.at[far_ref[c, j] >> 3, pl.ds(0, ROWS)], picked_ref.at[c * FAR + j], sem
            ).start()
    copy.wait()
    pltpu.make_async_copy(picked_ref, picked_ref, sem).wait()
    for pair in range(PAIRS):
        clusters = (2 * pair, 2 * pair + 1)
        blocks = [[picked_ref[c * FAR + j] for j in range(FAR)] for c in clusters]
        halves = [
            [
                ((far_ref[c, j] & 7) != low_ref[0, far_ref[c, j] >> 3]).astype(jnp.int32)
                for j in range(FAR)
            ]
            for c in clusters
        ]
        out_ref[pair] = field_pair(turned(skel_ref, pair), blocks, halves)


def far_one_field(far_one, low, arrived, skeleton_one):
    return pl.pallas_call(
        far_one_kernel,
        out_shape=jax.ShapeDtypeStruct((PAIRS, NRHS, 2 * RANK), jnp.float32),
        in_specs=[SM, SM, ANY, ANY],
        out_specs=VM,
        scratch_shapes=[
            bf16(DIM, ONE * RANK),
            bf16(ONE * FAR, ROWS, 2 * RANK),
            pltpu.SemaphoreType.DMA,
            pltpu.SemaphoreType.DMA((1,)),
        ],
        compiler_params=vmem(),
        cost_estimate=cost(1 << 28, 2 * MIB, 1 << 19),
        name="far_one_field",
    )(far_one, low, arrived, skeleton_one)


def final_kernel(
    far_ref, mine_ref, theirs_ref, field_one_hbm, skel_hbm, one_hbm, two_hbm, basis_hbm, near_hbm,
    out_ref, field_one_ref, skel_ref, one_ref, two_ref, basis_ref, near_ref, picked_ref, sem, in_sem,
):
    core = lax.rem(lax.axis_index("leaf"), 2)
    copies = fetch(
        in_sem, (skel_hbm, skel_ref), (field_one_hbm, field_one_ref), (one_hbm, one_ref),
        (two_hbm, two_ref), (basis_hbm, basis_ref), (near_hbm, near_ref),
    )
    for e in range(TWO):
        for j in range(FAR):
            b = far_ref[e, j]
            place = picked_ref.at[e * FAR + j]

            @pl.when((b & 1) == core)
            def _():
                pltpu.make_async_copy(mine_ref.at[b >> 1], place, sem).start()

            @pl.when((b & 1) != core)
            def _():
                pltpu.make_async_copy(theirs_ref.at[b >> 1], place, sem).start()

    for copy in copies:
        copy.wait()
    pltpu.make_async_copy(picked_ref, picked_ref, sem).wait()

    def split(x):
        high = x.astype(jnp.bfloat16)
        return jnp.concatenate([high, (x - high.astype(jnp.float32)).astype(jnp.bfloat16)], axis=0)

    def exact(parts, b):
        both = dot(parts, b)
        return both[:NRHS] + both[NRHS:]

    def whole(at):
        rows = picked_ref[at].astype(jnp.float32)
        return jnp.concatenate([rows, pltpu.roll(rows, RANK, 1)], axis=0).astype(jnp.bfloat16)

    blocks = [[whole(e * FAR + j) for j in range(FAR)] for e in range(TWO)]
    field_two = split(field_pair(turned(skel_ref, 0), blocks, [[0] * FAR] * TWO))
    from_two = [
        exact(field_two, padded(two_ref[e])) for e, padded in enumerate((upper, below))
    ]
    for pair in range(PAIRS):
        parent = from_two[pair // 2][:, (pair % 2) * 2 * RANK : (pair % 2 + 1) * 2 * RANK]
        down_one = split(field_one_ref[pair] + parent)
        for i, padded in enumerate((upper, below)):
            c = 2 * pair + i
            down_leaf = exact(down_one, padded(one_ref[c])).astype(jnp.bfloat16)
            for leaf in range(4):
                columns = pl.ds((4 * c + leaf) * LEAF, LEAF)
                half = down_leaf[:, (leaf // 2) * 2 * RANK : (leaf // 2 + 1) * 2 * RANK]
                basis = (upper, below)[leaf % 2](basis_ref[:, columns])
                out_ref[:, columns] = (near_ref[:, columns] + dot(half, basis)).astype(
                    jnp.bfloat16
                )


def finish(far_two, mine, theirs, field_one, skeleton_two, transfer_one, transfer_two, basis, near):
    scratch = (field_one, skeleton_two, transfer_one, transfer_two, basis, near)
    return pl.pallas_call(
        final_kernel,
        out_shape=jax.ShapeDtypeStruct((NRHS, LEAVES * LEAF), jnp.bfloat16),
        in_specs=[SM] + [ANY] * 8,
        out_specs=VM,
        scratch_shapes=[pltpu.VMEM(a.shape, a.dtype) for a in scratch]
        + [
            bf16(TWO * FAR, HALF_ROWS, 2 * RANK),
            pltpu.SemaphoreType.DMA,
            pltpu.SemaphoreType.DMA((6,)),
        ],
        compiler_params=vmem(),
        cost_estimate=cost(1 << 28, 3 * MIB, 1 << 17),
        name="finish",
    )(far_two, mine, theirs, *scratch)


def shift(x, step):
    return lax.ppermute(x, "leaf", [(i, (i + step) % PEERS) for i in range(PEERS)])


def swap(x):
    return lax.ppermute(x, "leaf", [(i, i ^ 1) for i in range(PEERS)])


def exchange(x):
    return lax.all_to_all(x, "leaf", split_axis=0, concat_axis=0, tiled=True)


def local(
    points, rhs, basis, transfer_one, transfer_two, skeleton_one, skeleton_two, near_source,
    far_one, far_two,
):
    me = lax.axis_index("leaf")
    wanted, low = ask(far_one)
    asked = exchange(wanted.reshape(PEERS, 1, PEERS)).reshape(PEERS, PEERS)
    message, to_right, to_left, own = pack(near_source, points, rhs)
    message, asked = lax.optimization_barrier((message, asked))
    arrived = exchange(message)
    from_left, from_right = shift(to_right, 1), shift(to_left, -1)
    columns = coefficients(rhs, basis, transfer_one, transfer_two, skeleton_one, skeleton_two)
    far_message = far_pack(asked[:, :2].reshape(-1), columns)
    field, lists = own_pairs(table_rows(near_source, me), own)
    far_message, arrived = lax.optimization_barrier((far_message, arrived))
    far_arrived = exchange(far_message)
    near = remote_pairs(
        lists, arrived.reshape(2 * PEERS, ROWS, LEAF), from_left, from_right, own, field
    )
    mine = far_arrived[:, ROWS:, :]
    theirs = swap(mine)
    field_one = far_one_field(far_one, low, far_arrived, skeleton_one)
    return finish(far_two, mine, theirs, field_one, skeleton_two, transfer_one, transfer_two,
                  basis, near)


def solution(mesh):
    placed = (
        P(None, "leaf"),
        P(None, "leaf"),
        P(None, "leaf"),
        P("leaf", None, None),
        P("leaf", None, None),
        P(None, "leaf"),
        P(None, "leaf"),
        P(),
        P("leaf", None),
        P("leaf", None),
    )
    return jax.shard_map(
        local, mesh=mesh, in_specs=placed, out_specs=P(None, "leaf"), check_vma=False
    )
```

```python
import jax
import jax.numpy as jnp
from jax import lax
from jax.experimental import pallas as pl
from jax.experimental.pallas import tpu as pltpu
from jax.sharding import PartitionSpec as P

DIM = 32
NRHS = 16
RANK = 64
LEAF = 256
NEAR = 10
FAR = 8
LEAVES = 32
ONE = 8
TWO = 2
PAIRS = ONE // 2
ROWS = DIM + NRHS
PEERS = 128
LOCAL = 2 * PEERS + 4
TABLE = LOCAL + LEAVES
GROUP = 16
LIST = 384
STRIDE = 512
HALF_ROWS = ROWS // 2
MESSAGE = ROWS + HALF_ROWS
MIB = 1 << 20

NT = (((1,), (1,)), ((), ()))
NN = (((1,), (0,)), ((), ()))


def dot(a, b, dims=NN):
    return lax.dot_general(a, b, dims, preferred_element_type=jnp.float32)


def vmem(limit=56):
    return pltpu.CompilerParams(vmem_limit_bytes=limit * MIB)


def cost(flops, moved, exps=0):
    return pl.CostEstimate(flops=flops, bytes_accessed=moved, transcendentals=exps)


def fetch(sem, *pairs):
    copies = [pltpu.make_async_copy(a, b, sem.at[i]) for i, (a, b) in enumerate(pairs)]
    for copy in copies:
        copy.start()
    return copies


def bf16(*shape):
    return pltpu.VMEM(shape, jnp.bfloat16)


ANY = pl.BlockSpec(memory_space=pl.ANY)
VM = pl.BlockSpec(memory_space=pltpu.VMEM)
SM = pl.BlockSpec(memory_space=pltpu.SMEM)


def ask_kernel(far_ref, ask_ref, low_ref):
    peer = lax.broadcasted_iota(jnp.int32, (PEERS, FAR), 0) * ONE
    low = high = None
    for i in range(ONE):
        at = far_ref[i : i + 1, :] - peer
        inside = (at >> 3) == 0
        a, b = jnp.where(inside, at, ONE), jnp.where(inside, at, -1)
        low = a if i == 0 else jnp.minimum(low, a)
        high = b if i == 0 else jnp.maximum(high, b)
    low = jnp.min(low.astype(jnp.float32), axis=1, keepdims=True)
    high = jnp.max(high.astype(jnp.float32), axis=1, keepdims=True)
    lane = lax.broadcasted_iota(jnp.int32, (PEERS, PEERS), 1)
    ask_ref[...] = jnp.where(lane == 0, low, high).astype(jnp.int32)
    across = lax.broadcasted_iota(jnp.int32, (ONE, PEERS), 1) * ONE
    low = None
    for j in range(FAR):
        at = far_ref[:, j : j + 1] - across
        a = jnp.where((at >> 3) == 0, at, ONE)
        low = a if j == 0 else jnp.minimum(low, a)
    low = jnp.min(low.astype(jnp.float32), axis=0, keepdims=True)
    low_ref[...] = jnp.broadcast_to(low, (ONE, PEERS)).astype(jnp.int32)


def ask(far_one):
    return pl.pallas_call(
        ask_kernel,
        out_shape=(
            jax.ShapeDtypeStruct((PEERS, PEERS), jnp.int32),
            jax.ShapeDtypeStruct((ONE, PEERS), jnp.int32),
        ),
        in_specs=[VM],
        out_specs=(VM, VM),
        compiler_params=vmem(),
        name="ask",
    )(far_one)


def pack_kernel(
    source_ref, points_ref, rhs_ref, msg_ref, right_ref, left_ref, own_ref,
    lists_ref, block_ref, row_ref, row_smem, in_sem, row_sem, msg_sem, side_sem,
):
    me = lax.axis_index("leaf")
    listed = pltpu.make_async_copy(source_ref, lists_ref, row_sem)
    listed.start()
    filled = fetch(
        in_sem,
        *(
            (ref.at[:, pl.ds(leaf * LEAF, LEAF)], block_ref.at[leaf, rows])
            for leaf in range(LEAVES)
            for ref, rows in ((points_ref, pl.ds(0, DIM)), (rhs_ref, pl.ds(DIM, NRHS)))
        ),
    )
    listed.wait()
    width = PEERS * LEAVES
    low = high = bits = None
    for k in range(NEAR):
        mine = lists_ref[k : k + 1, :] - me * LEAVES
        inside = (mine >> 5) == 0
        a = jnp.where(inside, mine, LEAVES)
        b = jnp.where(inside, mine, -1)
        c = jnp.where(inside, 1 << (mine & 31), 0)
        low = a if k == 0 else jnp.minimum(low, a)
        high = b if k == 0 else jnp.maximum(high, b)
        bits = c if k == 0 else bits | c
    low, high, bits = (jnp.broadcast_to(v, (8, width)) for v in (low, high, bits))
    for step in (16, 8, 4, 2, 1):
        low = jnp.minimum(low, pltpu.roll(low, width - step, 1))
        high = jnp.maximum(high, pltpu.roll(high, width - step, 1))
        bits = bits | pltpu.roll(bits, width - step, 1)
    place = lax.broadcasted_iota(jnp.int32, (8, width), 1) & 31
    row_ref[...] = jnp.where(
        place == 0, low, jnp.where(place == 1, pltpu.roll(high, 1, 1), pltpu.roll(bits, 2, 1))
    )
    copy = pltpu.make_async_copy(row_ref.at[0:1], row_smem, row_sem)
    copy.start()
    for fill in filled:
        fill.wait()
    own = pltpu.make_async_copy(block_ref, own_ref, in_sem.at[0])
    own.start()
    copy.wait()

    def send(peer, _):
        for slot in range(2):
            leaf = row_smem[0, peer * LEAVES + slot] & 31
            pltpu.make_async_copy(block_ref.at[leaf], msg_ref.at[peer, slot], msg_sem).start()
        return 0

    lax.fori_loop(0, PEERS, send, 0, unroll=4)
    for side, (ref, step) in enumerate(((right_ref, 1), (left_ref, PEERS - 1))):
        at = lax.rem(me + step, PEERS) * LEAVES
        between = row_smem[0, at + 2]
        between = between & ~(1 << (row_smem[0, at] & 31)) & ~(1 << (row_smem[0, at + 1] & 31))

        def scan(bit, found):
            has = ((between >> bit) & 1) == 1
            return jnp.where(has & (found[0] < 0), bit, found[0]), jnp.where(has, bit, found[1])

        first, last = lax.fori_loop(0, LEAVES, scan, (jnp.int32(-1), jnp.int32(0)))
        for slot, leaf in enumerate((first & 31, last & 31)):
            pltpu.make_async_copy(block_ref.at[leaf], ref.at[slot], side_sem.at[side]).start()
    pltpu.make_async_copy(msg_ref, msg_ref, msg_sem).wait()
    for side, ref in enumerate((right_ref, left_ref)):
        pltpu.make_async_copy(ref, ref, side_sem.at[side]).wait()
    own.wait()


def pack(source, points, rhs):
    block = jax.ShapeDtypeStruct((LEAVES, ROWS, LEAF), jnp.bfloat16)
    side = jax.ShapeDtypeStruct((2, ROWS, LEAF), jnp.bfloat16)
    return pl.pallas_call(
        pack_kernel,
        out_shape=(
            jax.ShapeDtypeStruct((PEERS, 2, ROWS, LEAF), jnp.bfloat16), side, side, block,
        ),
        in_specs=[ANY, ANY, ANY],
        out_specs=(ANY, ANY, ANY, ANY),
        scratch_shapes=[
            pltpu.VMEM((NEAR, PEERS * LEAVES), jnp.int32),
            bf16(LEAVES, ROWS, LEAF),
            pltpu.VMEM((8, PEERS * LEAVES), jnp.int32),
            pltpu.SMEM((1, PEERS * LEAVES), jnp.int32),
            pltpu.SemaphoreType.DMA((2 * LEAVES,)),
            pltpu.SemaphoreType.DMA,
            pltpu.SemaphoreType.DMA,
            pltpu.SemaphoreType.DMA((2,)),
        ],
        compiler_params=vmem(),
        cost_estimate=cost(1 << 20, 14 * MIB),
        name="pack",
    )(source.T, points, rhs)


def upper(b):
    return jnp.concatenate([b, jnp.zeros_like(b)], axis=0)


def below(b):
    return jnp.concatenate([jnp.zeros_like(b), b], axis=0)


def coeff_kernel(
    rhs_hbm, basis_hbm, one_hbm, two_hbm, skel_one_hbm, skel_two_hbm, out_ref,
    rhs_ref, basis_ref, one_ref, two_ref, skel_one_ref, skel_two_ref, sem,
):
    for copy in fetch(
        sem, (rhs_hbm, rhs_ref), (basis_hbm, basis_ref), (one_hbm, one_ref), (two_hbm, two_ref),
        (skel_one_hbm, skel_one_ref), (skel_two_hbm, skel_two_ref),
    ):
        copy.wait()

    def leaf_pair(leaf):
        a, b = (pl.ds((leaf + i) * LEAF, LEAF) for i in range(2))
        return (
            dot(rhs_ref[:, a], upper(basis_ref[:, a]), NT)
            + dot(rhs_ref[:, b], below(basis_ref[:, b]), NT)
        ).astype(jnp.bfloat16)

    def lift_pair(children, transfer_ref, cluster):
        return (
            dot(children[0], upper(transfer_ref[cluster]), NT)
            + dot(children[1], below(transfer_ref[cluster + 1]), NT)
        ).astype(jnp.bfloat16)

    pairs = []
    for pair in range(PAIRS):
        joined = [
            jnp.concatenate([leaf_pair(4 * c), leaf_pair(4 * c + 2)], axis=1)
            for c in (2 * pair, 2 * pair + 1)
        ]
        pairs.append(lift_pair(joined, one_ref, 2 * pair))
        out_ref[pair, :DIM, :] = skel_one_ref[:, pl.ds(pair * 2 * RANK, 2 * RANK)]
        out_ref[pair, DIM:, :] = pairs[-1]
    joined = [jnp.concatenate(pairs[2 * e : 2 * e + 2], axis=1) for e in range(TWO)]
    out_ref[PAIRS, :DIM, :] = skel_two_ref[...]
    out_ref[PAIRS, DIM:, :] = lift_pair(joined, two_ref, 0)


def coefficients(*args):
    return pl.pallas_call(
        coeff_kernel,
        out_shape=jax.ShapeDtypeStruct((PAIRS + 1, ROWS, 2 * RANK), jnp.bfloat16),
        in_specs=[ANY] * 6,
        out_specs=VM,
        scratch_shapes=[bf16(*a.shape) for a in args] + [pltpu.SemaphoreType.DMA((6,))],
        compiler_params=vmem(),
        cost_estimate=cost(1 << 26, 2 * MIB),
        name="coefficients",
    )(*args)


def far_pack_kernel(asked_ref, columns_ref, out_ref, low_ref, high_ref):
    left = lax.broadcasted_iota(jnp.int32, (ROWS, 2 * RANK), 1) < RANK
    for pair in range(PAIRS):
        wide = columns_ref[pair].astype(jnp.float32)
        turned = pltpu.roll(wide, RANK, 1)
        low_ref[2 * pair] = high_ref[2 * pair + 1] = wide
        low_ref[2 * pair + 1] = high_ref[2 * pair] = turned
    wide = columns_ref[PAIRS].astype(jnp.float32)
    turned = pltpu.roll(wide, RANK, 1)
    half = left[:HALF_ROWS]
    second = (
        jnp.where(half, wide[:HALF_ROWS], turned[HALF_ROWS:]),
        jnp.where(half, turned[:HALF_ROWS], wide[HALF_ROWS:]),
    )

    def fill(chip, _):
        for core in range(2):
            peer = 2 * chip + core
            first = jnp.where(
                left, low_ref[asked_ref[2 * peer] & 7], high_ref[asked_ref[2 * peer + 1] & 7]
            )
            out_ref[peer] = jnp.concatenate([first, second[core]], axis=0).astype(jnp.bfloat16)
        return 0

    lax.fori_loop(0, PEERS // 2, fill, 0, unroll=2)


def far_pack(asked, columns):
    return pl.pallas_call(
        far_pack_kernel,
        out_shape=jax.ShapeDtypeStruct((PEERS, MESSAGE, 2 * RANK), jnp.bfloat16),
        in_specs=[SM, VM],
        out_specs=VM,
        scratch_shapes=[pltpu.VMEM((ONE, ROWS, 2 * RANK), jnp.float32)] * 2,
        compiler_params=vmem(),
        cost_estimate=cost(1 << 20, 5 * MIB),
        name="far_pack",
    )(asked, columns)


def table_rows(near_source, me):
    mine = lax.dynamic_slice_in_dim(near_source, me * LEAVES, LEAVES, 0).reshape(-1)
    device, leaf = mine >> 5, mine & 31
    from_peer = device[:, None] == jnp.arange(PEERS, dtype=jnp.int32)[None, :]
    low = jnp.min(jnp.where(from_peer, leaf[:, None], LEAVES), axis=0)
    high = jnp.max(jnp.where(from_peer, leaf[:, None], -1), axis=0)
    low_of = jnp.sum(jnp.where(from_peer, low[None, :], 0), axis=1)
    high_of = jnp.sum(jnp.where(from_peer, high[None, :], 0), axis=1)
    row = 2 * device + (leaf != low_of)
    inner = (leaf > low_of) & (leaf < high_of)
    for side, step in enumerate((PEERS - 1, 1)):
        chosen = inner & (device == (me + step) % PEERS)
        first = jnp.min(jnp.where(chosen, leaf, LEAVES))
        row = jnp.where(chosen, 2 * PEERS + 2 * side + (leaf != first), row)
    return jnp.where(device == me, LOCAL + leaf, row)


def with_square(block, first):
    wide = block.astype(jnp.float32)
    square = jnp.sum(wide * wide, axis=0, keepdims=True) * -2
    high = square.astype(jnp.bfloat16).astype(jnp.float32)
    middle = (square - high).astype(jnp.bfloat16).astype(jnp.float32)
    low = square - high - middle
    at = lax.broadcasted_iota(jnp.int32, (16, LEAF), 0)
    ones, parts = (3, 0) if first else (0, 3)
    extra = jnp.where((at >= ones) & (at < ones + 3), 1.0, 0.0)
    for i, part in enumerate((high, middle, low)):
        extra = jnp.where(at == parts + i, part, extra)
    if first:
        return jnp.concatenate([wide * 4, extra], axis=0).T.astype(jnp.bfloat16)
    return jnp.concatenate([block, extra.astype(jnp.bfloat16)], axis=0)


def turn_targets(own_ref, target_ref):
    def turn(leaf, _):
        target_ref[leaf, :, :ROWS] = with_square(own_ref[leaf, :DIM, :], True)
        return 0

    lax.fori_loop(0, LEAVES, turn, 0, unroll=2)


def add_pairs(list_ref, start, table_ref, target_ref, out_ref):
    def step(i, _):
        terms = []
        for u in range(GROUP):
            pair = list_ref[start + i * GROUP + u]
            target, row = pair // STRIDE, pair & (STRIDE - 1)
            weights = jnp.exp(
                dot(target_ref[target, :, :ROWS], with_square(table_ref[row, :DIM, :], False))
            ).astype(jnp.bfloat16)
            terms.append((target, dot(table_ref[row, DIM:, :], weights, NT)))
        for target, term in terms:
            columns = pl.ds(pl.multiple_of(target * LEAF, LEAF), LEAF)
            out_ref[:, columns] += term
        return 0

    lax.fori_loop(0, (list_ref[start + LIST - 1] + GROUP - 1) // GROUP, step, 0)


def own_kernel(row_ref, own_hbm, out_ref, list_ref, own_ref, target_ref, sem):
    (copy,) = fetch(sem, (own_hbm, own_ref.at[pl.ds(0, LEAVES)]))

    def sort(target, counts):
        mine, others = counts
        for k in range(NEAR):
            row = row_ref[target * NEAR + k]
            list_ref[mine] = target * STRIDE + jnp.maximum(row - LOCAL, 0)
            list_ref[LIST + others] = target * STRIDE + row
            is_mine = (row >= LOCAL).astype(jnp.int32)
            mine, others = mine + is_mine, others + 1 - is_mine
        return mine, others

    mine, others = lax.fori_loop(0, LEAVES, sort, (jnp.int32(0), jnp.int32(0)))
    for u in range(GROUP):
        list_ref[mine + u] = LEAVES
        list_ref[LIST + others + u] = LOCAL
    list_ref[LIST - 1] = mine
    list_ref[2 * LIST - 1] = others
    own_ref[LEAVES] = jnp.zeros((ROWS, LEAF), jnp.bfloat16)
    copy.wait()
    turn_targets(own_ref, target_ref)
    out_ref[...] = jnp.zeros_like(out_ref)
    add_pairs(list_ref, 0, own_ref, target_ref, out_ref)


def own_pairs(rows, own):
    return pl.pallas_call(
        own_kernel,
        out_shape=(
            jax.ShapeDtypeStruct((NRHS, LEAVES * LEAF), jnp.float32),
            jax.ShapeDtypeStruct((2 * LIST,), jnp.int32),
        ),
        in_specs=[SM, ANY],
        out_specs=(VM, SM),
        scratch_shapes=[
            bf16(LEAVES + 1, ROWS, LEAF),
            bf16(LEAVES, LEAF, 128),
            pltpu.SemaphoreType.DMA((1,)),
        ],
        compiler_params=vmem(),
        cost_estimate=cost(2 * 120 * 65536 * 272, 2 * MIB, 120 * 65536),
        name="own_pairs",
    )(rows, own)


def remote_kernel(
    list_ref, arrived_ref, left_ref, right_ref, own_hbm, field_ref, out_ref,
    table_ref, own_ref, target_ref, sem,
):
    near = fetch(
        sem,
        (own_hbm, own_ref),
        (field_ref, out_ref),
        (arrived_ref, table_ref.at[pl.ds(0, 2 * PEERS)]),
        (left_ref, table_ref.at[pl.ds(2 * PEERS, 2)]),
        (right_ref, table_ref.at[pl.ds(2 * PEERS + 2, 2)]),
    )
    table_ref[LOCAL] = jnp.zeros((ROWS, LEAF), jnp.bfloat16)
    near[0].wait()
    turn_targets(own_ref, target_ref)
    for copy in near[1:]:
        copy.wait()
    add_pairs(list_ref, LIST, table_ref, target_ref, out_ref)


def remote_pairs(lists, arrived, left, right, own, field):
    return pl.pallas_call(
        remote_kernel,
        out_shape=jax.ShapeDtypeStruct((NRHS, LEAVES * LEAF), jnp.float32),
        in_specs=[SM, ANY, ANY, ANY, ANY, ANY],
        out_specs=VM,
        scratch_shapes=[
            bf16(LOCAL + 1, ROWS, LEAF),
            bf16(LEAVES, ROWS, LEAF),
            bf16(LEAVES, LEAF, 128),
            pltpu.SemaphoreType.DMA((5,)),
        ],
        compiler_params=vmem(),
        cost_estimate=cost(2 * 200 * 65536 * 272, 8 * MIB, 200 * 65536),
        name="remote_pairs",
    )(lists, arrived, left, right, own, field)


def turned(skel_ref, pair):
    return skel_ref[:, pl.ds(pair * 2 * RANK, 2 * RANK)].astype(jnp.float32).T


def field_pair(targets, blocks, halves):
    half_of = lax.broadcasted_iota(jnp.int32, (NRHS, 2 * RANK), 1) >> 6
    total = None
    for i, padded in enumerate((upper, below)):
        target = targets[i * RANK : (i + 1) * RANK]
        target_sq = jnp.sum(target * target, axis=1, keepdims=True) * 2
        source = jnp.concatenate([block[:DIM] for block in blocks[i]], axis=1)
        coeffs = jnp.concatenate(
            [
                jnp.where(half_of == half, block[DIM:], 0)
                for block, half in zip(blocks[i], halves[i], strict=True)
            ],
            axis=1,
        )
        wide = source.astype(jnp.float32)
        source_sq = jnp.sum(wide * wide, axis=0, keepdims=True) * 2
        power = dot((target * 4).astype(jnp.bfloat16), source) - target_sq - source_sq
        weights = jnp.exp(power).astype(jnp.bfloat16)
        term = dot(coeffs, padded(weights), NT)
        total = term if i == 0 else total + term
    return total


def far_one_kernel(far_ref, low_ref, arrived_ref, skel_hbm, out_ref, skel_ref, picked_ref, sem, in_sem):
    (copy,) = fetch(in_sem, (skel_hbm, skel_ref))
    for c in range(ONE):
        for j in range(FAR):
            pltpu.make_async_copy(
                arrived_ref.at[far_ref[c, j] >> 3, pl.ds(0, ROWS)], picked_ref.at[c * FAR + j], sem
            ).start()
    copy.wait()
    pltpu.make_async_copy(picked_ref, picked_ref, sem).wait()
    for pair in range(PAIRS):
        clusters = (2 * pair, 2 * pair + 1)
        blocks = [[picked_ref[c * FAR + j] for j in range(FAR)] for c in clusters]
        halves = [
            [
                ((far_ref[c, j] & 7) != low_ref[0, far_ref[c, j] >> 3]).astype(jnp.int32)
                for j in range(FAR)
            ]
            for c in clusters
        ]
        out_ref[pair] = field_pair(turned(skel_ref, pair), blocks, halves)


def far_one_field(far_one, low, arrived, skeleton_one):
    return pl.pallas_call(
        far_one_kernel,
        out_shape=jax.ShapeDtypeStruct((PAIRS, NRHS, 2 * RANK), jnp.float32),
        in_specs=[SM, SM, ANY, ANY],
        out_specs=VM,
        scratch_shapes=[
            bf16(DIM, ONE * RANK),
            bf16(ONE * FAR, ROWS, 2 * RANK),
            pltpu.SemaphoreType.DMA,
            pltpu.SemaphoreType.DMA((1,)),
        ],
        compiler_params=vmem(),
        cost_estimate=cost(1 << 28, 2 * MIB, 1 << 19),
        name="far_one_field",
    )(far_one, low, arrived, skeleton_one)


def final_kernel(
    far_ref, mine_ref, theirs_ref, field_one_hbm, skel_hbm, one_hbm, two_hbm, basis_hbm, near_hbm,
    out_ref, field_one_ref, skel_ref, one_ref, two_ref, basis_ref, near_ref, picked_ref, sem, in_sem,
):
    core = lax.rem(lax.axis_index("leaf"), 2)
    copies = fetch(
        in_sem, (skel_hbm, skel_ref), (field_one_hbm, field_one_ref), (one_hbm, one_ref),
        (two_hbm, two_ref), (basis_hbm, basis_ref), (near_hbm, near_ref),
    )
    for e in range(TWO):
        for j in range(FAR):
            b = far_ref[e, j]
            place = picked_ref.at[e * FAR + j]

            @pl.when((b & 1) == core)
            def _():
                pltpu.make_async_copy(mine_ref.at[b >> 1], place, sem).start()

            @pl.when((b & 1) != core)
            def _():
                pltpu.make_async_copy(theirs_ref.at[b >> 1], place, sem).start()

    for copy in copies:
        copy.wait()
    pltpu.make_async_copy(picked_ref, picked_ref, sem).wait()

    def split(x):
        high = x.astype(jnp.bfloat16)
        return jnp.concatenate([high, (x - high.astype(jnp.float32)).astype(jnp.bfloat16)], axis=0)

    def exact(parts, b):
        both = dot(parts, b)
        return both[:NRHS] + both[NRHS:]

    def whole(at):
        rows = picked_ref[at].astype(jnp.float32)
        return jnp.concatenate([rows, pltpu.roll(rows, RANK, 1)], axis=0).astype(jnp.bfloat16)

    blocks = [[whole(e * FAR + j) for j in range(FAR)] for e in range(TWO)]
    field_two = split(field_pair(turned(skel_ref, 0), blocks, [[0] * FAR] * TWO))
    from_two = [
        exact(field_two, padded(two_ref[e])) for e, padded in enumerate((upper, below))
    ]
    for pair in range(PAIRS):
        parent = from_two[pair // 2][:, (pair % 2) * 2 * RANK : (pair % 2 + 1) * 2 * RANK]
        down_one = split(field_one_ref[pair] + parent)
        for i, padded in enumerate((upper, below)):
            c = 2 * pair + i
            down_leaf = exact(down_one, padded(one_ref[c])).astype(jnp.bfloat16)
            for leaf in range(4):
                columns = pl.ds((4 * c + leaf) * LEAF, LEAF)
                half = down_leaf[:, (leaf // 2) * 2 * RANK : (leaf // 2 + 1) * 2 * RANK]
                basis = (upper, below)[leaf % 2](basis_ref[:, columns])
                out_ref[:, columns] = (near_ref[:, columns] + dot(half, basis)).astype(
                    jnp.bfloat16
                )


def finish(far_two, mine, theirs, field_one, skeleton_two, transfer_one, transfer_two, basis, near):
    scratch = (field_one, skeleton_two, transfer_one, transfer_two, basis, near)
    return pl.pallas_call(
        final_kernel,
        out_shape=jax.ShapeDtypeStruct((NRHS, LEAVES * LEAF), jnp.bfloat16),
        in_specs=[SM] + [ANY] * 8,
        out_specs=VM,
        scratch_shapes=[pltpu.VMEM(a.shape, a.dtype) for a in scratch]
        + [
            bf16(TWO * FAR, HALF_ROWS, 2 * RANK),
            pltpu.SemaphoreType.DMA,
            pltpu.SemaphoreType.DMA((6,)),
        ],
        compiler_params=vmem(),
        cost_estimate=cost(1 << 28, 3 * MIB, 1 << 17),
        name="finish",
    )(far_two, mine, theirs, *scratch)


def shift(x, step):
    return lax.ppermute(x, "leaf", [(i, (i + step) % PEERS) for i in range(PEERS)])


def swap(x):
    return lax.ppermute(x, "leaf", [(i, i ^ 1) for i in range(PEERS)])


def exchange(x):
    return lax.all_to_all(x, "leaf", split_axis=0, concat_axis=0, tiled=True)


def local(
    points, rhs, basis, transfer_one, transfer_two, skeleton_one, skeleton_two, near_source,
    far_one, far_two,
):
    me = lax.axis_index("leaf")
    wanted, low = ask(far_one)
    asked = exchange(wanted.reshape(PEERS, 1, PEERS)).reshape(PEERS, PEERS)
    message, to_right, to_left, own = pack(near_source, points, rhs)
    message, asked = lax.optimization_barrier((message, asked))
    arrived = exchange(message)
    columns = coefficients(rhs, basis, transfer_one, transfer_two, skeleton_one, skeleton_two)
    far_message = far_pack(asked[:, :2].reshape(-1), columns)
    field, lists = own_pairs(table_rows(near_source, me), own)
    to_right, to_left, far_message, field, lists = lax.optimization_barrier(
        (to_right, to_left, far_message, field, lists)
    )
    from_left, from_right = shift(to_right, 1), shift(to_left, -1)
    far_message, arrived, from_left, from_right = lax.optimization_barrier(
        (far_message, arrived, from_left, from_right)
    )
    far_arrived = exchange(far_message)
    near = remote_pairs(
        lists, arrived.reshape(2 * PEERS, ROWS, LEAF), from_left, from_right, own, field
    )
    far_arrived, near = lax.optimization_barrier((far_arrived, near))
    mine = far_arrived[:, ROWS:, :]
    theirs = swap(mine)
    field_one = far_one_field(far_one, low, far_arrived, skeleton_one)
    return finish(far_two, mine, theirs, field_one, skeleton_two, transfer_one, transfer_two,
                  basis, near)


def solution(mesh):
    placed = (
        P(None, "leaf"),
        P(None, "leaf"),
        P(None, "leaf"),
        P("leaf", None, None),
        P("leaf", None, None),
        P(None, "leaf"),
        P(None, "leaf"),
        P(),
        P("leaf", None),
        P("leaf", None),
    )
    return jax.shard_map(
        local, mesh=mesh, in_specs=placed, out_specs=P(None, "leaf"), check_vma=False
    )
```

```python
import jax
import jax.numpy as jnp
from jax import lax
from jax.experimental import pallas as pl
from jax.experimental.pallas import tpu as pltpu
from jax.sharding import PartitionSpec as P

DIM = 32
NRHS = 16
RANK = 64
LEAF = 256
NEAR = 10
FAR = 8
LEAVES = 32
ONE = 8
TWO = 2
PAIRS = ONE // 2
ROWS = DIM + NRHS
PEERS = 128
LOCAL = 2 * PEERS + 4
TABLE = LOCAL + LEAVES
GROUP = 16
LIST = 384
STRIDE = 512
HALF_ROWS = ROWS // 2
MESSAGE = ROWS + HALF_ROWS
MIB = 1 << 20

NT = (((1,), (1,)), ((), ()))
NN = (((1,), (0,)), ((), ()))


def dot(a, b, dims=NN):
    return lax.dot_general(a, b, dims, preferred_element_type=jnp.float32)


def vmem(limit):
    return pltpu.CompilerParams(vmem_limit_bytes=limit * MIB)


def cost(flops, moved, exps=0):
    return pl.CostEstimate(flops=flops, bytes_accessed=moved, transcendentals=exps)


def fetch(sem, *pairs):
    copies = [pltpu.make_async_copy(a, b, sem.at[i]) for i, (a, b) in enumerate(pairs)]
    for copy in copies:
        copy.start()
    return copies


def bf16(*shape):
    return pltpu.VMEM(shape, jnp.bfloat16)


ANY = pl.BlockSpec(memory_space=pl.ANY)
VM = pl.BlockSpec(memory_space=pltpu.VMEM)
SM = pl.BlockSpec(memory_space=pltpu.SMEM)


def ask_kernel(far_ref, ask_ref, low_ref):
    peer = lax.broadcasted_iota(jnp.int32, (PEERS, FAR), 0) * ONE
    low = high = None
    for i in range(ONE):
        at = far_ref[i : i + 1, :] - peer
        inside = (at >> 3) == 0
        a, b = jnp.where(inside, at, ONE), jnp.where(inside, at, -1)
        low = a if i == 0 else jnp.minimum(low, a)
        high = b if i == 0 else jnp.maximum(high, b)
    low = jnp.min(low.astype(jnp.float32), axis=1, keepdims=True)
    high = jnp.max(high.astype(jnp.float32), axis=1, keepdims=True)
    lane = lax.broadcasted_iota(jnp.int32, (PEERS, PEERS), 1)
    ask_ref[...] = jnp.where(lane == 0, low, high).astype(jnp.int32)
    across = lax.broadcasted_iota(jnp.int32, (ONE, PEERS), 1) * ONE
    low = None
    for j in range(FAR):
        at = far_ref[:, j : j + 1] - across
        a = jnp.where((at >> 3) == 0, at, ONE)
        low = a if j == 0 else jnp.minimum(low, a)
    low = jnp.min(low.astype(jnp.float32), axis=0, keepdims=True)
    low_ref[...] = jnp.broadcast_to(low, (ONE, PEERS)).astype(jnp.int32)


def ask(far_one):
    return pl.pallas_call(
        ask_kernel,
        out_shape=(
            jax.ShapeDtypeStruct((PEERS, PEERS), jnp.int32),
            jax.ShapeDtypeStruct((ONE, PEERS), jnp.int32),
        ),
        in_specs=[VM],
        out_specs=(VM, VM),
        compiler_params=vmem(8),
        name="ask",
    )(far_one)


def pack_kernel(
    source_ref, points_ref, rhs_ref, msg_ref, right_ref, left_ref, own_ref,
    lists_ref, block_ref, row_ref, row_smem, in_sem, row_sem, msg_sem, side_sem,
):
    me = lax.axis_index("leaf")
    listed = pltpu.make_async_copy(source_ref, lists_ref, row_sem)
    listed.start()
    filled = fetch(
        in_sem,
        *(
            (ref.at[:, pl.ds(leaf * LEAF, LEAF)], block_ref.at[leaf, rows])
            for leaf in range(LEAVES)
            for ref, rows in ((points_ref, pl.ds(0, DIM)), (rhs_ref, pl.ds(DIM, NRHS)))
        ),
    )
    listed.wait()
    width = PEERS * LEAVES
    low = high = bits = None
    for k in range(NEAR):
        mine = lists_ref[k : k + 1, :] - me * LEAVES
        inside = (mine >> 5) == 0
        a = jnp.where(inside, mine, LEAVES)
        b = jnp.where(inside, mine, -1)
        c = jnp.where(inside, 1 << (mine & 31), 0)
        low = a if k == 0 else jnp.minimum(low, a)
        high = b if k == 0 else jnp.maximum(high, b)
        bits = c if k == 0 else bits | c
    low, high, bits = (jnp.broadcast_to(v, (8, width)) for v in (low, high, bits))
    for step in (16, 8, 4, 2, 1):
        low = jnp.minimum(low, pltpu.roll(low, width - step, 1))
        high = jnp.maximum(high, pltpu.roll(high, width - step, 1))
        bits = bits | pltpu.roll(bits, width - step, 1)
    place = lax.broadcasted_iota(jnp.int32, (8, width), 1) & 31
    row_ref[...] = jnp.where(
        place == 0, low, jnp.where(place == 1, pltpu.roll(high, 1, 1), pltpu.roll(bits, 2, 1))
    )
    copy = pltpu.make_async_copy(row_ref.at[0:1], row_smem, row_sem)
    copy.start()
    for fill in filled:
        fill.wait()
    own = pltpu.make_async_copy(block_ref, own_ref, in_sem.at[0])
    own.start()
    copy.wait()

    def send(peer, _):
        for slot in range(2):
            leaf = row_smem[0, peer * LEAVES + slot] & 31
            pltpu.make_async_copy(block_ref.at[leaf], msg_ref.at[peer, slot], msg_sem).start()
        return 0

    lax.fori_loop(0, PEERS, send, 0, unroll=4)
    for side, (ref, step) in enumerate(((right_ref, 1), (left_ref, PEERS - 1))):
        at = lax.rem(me + step, PEERS) * LEAVES
        between = row_smem[0, at + 2]
        between = between & ~(1 << (row_smem[0, at] & 31)) & ~(1 << (row_smem[0, at + 1] & 31))

        def scan(bit, found):
            has = ((between >> bit) & 1) == 1
            return jnp.where(has & (found[0] < 0), bit, found[0]), jnp.where(has, bit, found[1])

        first, last = lax.fori_loop(0, LEAVES, scan, (jnp.int32(-1), jnp.int32(0)))
        for slot, leaf in enumerate((first & 31, last & 31)):
            pltpu.make_async_copy(block_ref.at[leaf], ref.at[slot], side_sem.at[side]).start()
    pltpu.make_async_copy(msg_ref, msg_ref, msg_sem).wait()
    for side, ref in enumerate((right_ref, left_ref)):
        pltpu.make_async_copy(ref, ref, side_sem.at[side]).wait()
    own.wait()


def pack(source, points, rhs):
    block = jax.ShapeDtypeStruct((LEAVES, ROWS, LEAF), jnp.bfloat16)
    side = jax.ShapeDtypeStruct((2, ROWS, LEAF), jnp.bfloat16)
    return pl.pallas_call(
        pack_kernel,
        out_shape=(
            jax.ShapeDtypeStruct((PEERS, 2, ROWS, LEAF), jnp.bfloat16), side, side, block,
        ),
        in_specs=[ANY, ANY, ANY],
        out_specs=(ANY, ANY, ANY, ANY),
        scratch_shapes=[
            pltpu.VMEM((NEAR, PEERS * LEAVES), jnp.int32),
            bf16(LEAVES, ROWS, LEAF),
            pltpu.VMEM((8, PEERS * LEAVES), jnp.int32),
            pltpu.SMEM((1, PEERS * LEAVES), jnp.int32),
            pltpu.SemaphoreType.DMA((2 * LEAVES,)),
            pltpu.SemaphoreType.DMA,
            pltpu.SemaphoreType.DMA,
            pltpu.SemaphoreType.DMA((2,)),
        ],
        compiler_params=vmem(56),
        cost_estimate=cost(1 << 20, 14 * MIB),
        name="pack",
    )(source.T, points, rhs)


def upper(b):
    return jnp.concatenate([b, jnp.zeros_like(b)], axis=0)


def below(b):
    return jnp.concatenate([jnp.zeros_like(b), b], axis=0)


def coeff_kernel(
    rhs_hbm, basis_hbm, one_hbm, two_hbm, skel_one_hbm, skel_two_hbm, out_ref,
    rhs_ref, basis_ref, one_ref, two_ref, skel_one_ref, skel_two_ref, sem,
):
    for copy in fetch(
        sem, (rhs_hbm, rhs_ref), (basis_hbm, basis_ref), (one_hbm, one_ref), (two_hbm, two_ref),
        (skel_one_hbm, skel_one_ref), (skel_two_hbm, skel_two_ref),
    ):
        copy.wait()

    def leaf_pair(leaf):
        a, b = (pl.ds((leaf + i) * LEAF, LEAF) for i in range(2))
        return (
            dot(rhs_ref[:, a], upper(basis_ref[:, a]), NT)
            + dot(rhs_ref[:, b], below(basis_ref[:, b]), NT)
        ).astype(jnp.bfloat16)

    def lift_pair(children, transfer_ref, cluster):
        return (
            dot(children[0], upper(transfer_ref[cluster]), NT)
            + dot(children[1], below(transfer_ref[cluster + 1]), NT)
        ).astype(jnp.bfloat16)

    pairs = []
    for pair in range(PAIRS):
        joined = [
            jnp.concatenate([leaf_pair(4 * c), leaf_pair(4 * c + 2)], axis=1)
            for c in (2 * pair, 2 * pair + 1)
        ]
        pairs.append(lift_pair(joined, one_ref, 2 * pair))
        out_ref[pair, :DIM, :] = skel_one_ref[:, pl.ds(pair * 2 * RANK, 2 * RANK)]
        out_ref[pair, DIM:, :] = pairs[-1]
    joined = [jnp.concatenate(pairs[2 * e : 2 * e + 2], axis=1) for e in range(TWO)]
    out_ref[PAIRS, :DIM, :] = skel_two_ref[...]
    out_ref[PAIRS, DIM:, :] = lift_pair(joined, two_ref, 0)


def coefficients(*args):
    return pl.pallas_call(
        coeff_kernel,
        out_shape=jax.ShapeDtypeStruct((PAIRS + 1, ROWS, 2 * RANK), jnp.bfloat16),
        in_specs=[ANY] * 6,
        out_specs=VM,
        scratch_shapes=[bf16(*a.shape) for a in args] + [pltpu.SemaphoreType.DMA((6,))],
        compiler_params=vmem(24),
        cost_estimate=cost(1 << 26, 2 * MIB),
        name="coefficients",
    )(*args)


def far_pack_kernel(asked_ref, columns_ref, out_ref, low_ref, high_ref):
    left = lax.broadcasted_iota(jnp.int32, (ROWS, 2 * RANK), 1) < RANK
    for pair in range(PAIRS):
        wide = columns_ref[pair].astype(jnp.float32)
        turned = pltpu.roll(wide, RANK, 1)
        low_ref[2 * pair] = high_ref[2 * pair + 1] = wide
        low_ref[2 * pair + 1] = high_ref[2 * pair] = turned
    wide = columns_ref[PAIRS].astype(jnp.float32)
    turned = pltpu.roll(wide, RANK, 1)
    half = left[:HALF_ROWS]
    second = (
        jnp.where(half, wide[:HALF_ROWS], turned[HALF_ROWS:]),
        jnp.where(half, turned[:HALF_ROWS], wide[HALF_ROWS:]),
    )

    def fill(chip, _):
        for core in range(2):
            peer = 2 * chip + core
            first = jnp.where(
                left, low_ref[asked_ref[2 * peer] & 7], high_ref[asked_ref[2 * peer + 1] & 7]
            )
            out_ref[peer] = jnp.concatenate([first, second[core]], axis=0).astype(jnp.bfloat16)
        return 0

    lax.fori_loop(0, PEERS // 2, fill, 0, unroll=2)


def far_pack(asked, columns):
    return pl.pallas_call(
        far_pack_kernel,
        out_shape=jax.ShapeDtypeStruct((PEERS, MESSAGE, 2 * RANK), jnp.bfloat16),
        in_specs=[SM, VM],
        out_specs=VM,
        scratch_shapes=[pltpu.VMEM((ONE, ROWS, 2 * RANK), jnp.float32)] * 2,
        compiler_params=vmem(16),
        cost_estimate=cost(1 << 20, 5 * MIB),
        name="far_pack",
    )(asked, columns)


def table_rows(near_source, me):
    mine = lax.dynamic_slice_in_dim(near_source, me * LEAVES, LEAVES, 0).reshape(-1)
    device, leaf = mine >> 5, mine & 31
    from_peer = device[:, None] == jnp.arange(PEERS, dtype=jnp.int32)[None, :]
    low = jnp.min(jnp.where(from_peer, leaf[:, None], LEAVES), axis=0)
    high = jnp.max(jnp.where(from_peer, leaf[:, None], -1), axis=0)
    low_of = jnp.sum(jnp.where(from_peer, low[None, :], 0), axis=1)
    high_of = jnp.sum(jnp.where(from_peer, high[None, :], 0), axis=1)
    row = 2 * device + (leaf != low_of)
    inner = (leaf > low_of) & (leaf < high_of)
    for side, step in enumerate((PEERS - 1, 1)):
        chosen = inner & (device == (me + step) % PEERS)
        first = jnp.min(jnp.where(chosen, leaf, LEAVES))
        row = jnp.where(chosen, 2 * PEERS + 2 * side + (leaf != first), row)
    return jnp.where(device == me, LOCAL + leaf, row)


def with_square(block, first):
    wide = block.astype(jnp.float32)
    square = jnp.sum(wide * wide, axis=0, keepdims=True) * -2
    high = square.astype(jnp.bfloat16).astype(jnp.float32)
    middle = (square - high).astype(jnp.bfloat16).astype(jnp.float32)
    low = square - high - middle
    at = lax.broadcasted_iota(jnp.int32, (16, LEAF), 0)
    ones, parts = (3, 0) if first else (0, 3)
    extra = jnp.where((at >= ones) & (at < ones + 3), 1.0, 0.0)
    for i, part in enumerate((high, middle, low)):
        extra = jnp.where(at == parts + i, part, extra)
    if first:
        return jnp.concatenate([wide * 4, extra], axis=0).T.astype(jnp.bfloat16)
    return jnp.concatenate([block, extra.astype(jnp.bfloat16)], axis=0)


def turn_targets(own_ref, target_ref):
    def turn(leaf, _):
        target_ref[leaf, :, :ROWS] = with_square(own_ref[leaf, :DIM, :], True)
        return 0

    lax.fori_loop(0, LEAVES, turn, 0, unroll=2)


def add_pairs(list_ref, start, table_ref, target_ref, out_ref):
    def step(i, _):
        terms = []
        for u in range(GROUP):
            pair = list_ref[start + i * GROUP + u]
            target, row = pair // STRIDE, pair & (STRIDE - 1)
            weights = jnp.exp(
                dot(target_ref[target, :, :ROWS], with_square(table_ref[row, :DIM, :], False))
            ).astype(jnp.bfloat16)
            terms.append((target, dot(table_ref[row, DIM:, :], weights, NT)))
        for target, term in terms:
            columns = pl.ds(pl.multiple_of(target * LEAF, LEAF), LEAF)
            out_ref[:, columns] += term
        return 0

    lax.fori_loop(0, (list_ref[start + LIST - 1] + GROUP - 1) // GROUP, step, 0)


def own_kernel(row_ref, own_hbm, out_ref, list_ref, own_ref, target_ref, sem):
    (copy,) = fetch(sem, (own_hbm, own_ref.at[pl.ds(0, LEAVES)]))

    def sort(target, counts):
        mine, others = counts
        for k in range(NEAR):
            row = row_ref[target * NEAR + k]
            list_ref[mine] = target * STRIDE + jnp.maximum(row - LOCAL, 0)
            list_ref[LIST + others] = target * STRIDE + row
            is_mine = (row >= LOCAL).astype(jnp.int32)
            mine, others = mine + is_mine, others + 1 - is_mine
        return mine, others

    mine, others = lax.fori_loop(0, LEAVES, sort, (jnp.int32(0), jnp.int32(0)))
    for u in range(GROUP):
        list_ref[mine + u] = LEAVES
        list_ref[LIST + others + u] = LOCAL
    list_ref[LIST - 1] = mine
    list_ref[2 * LIST - 1] = others
    own_ref[LEAVES] = jnp.zeros((ROWS, LEAF), jnp.bfloat16)
    copy.wait()
    turn_targets(own_ref, target_ref)
    out_ref[...] = jnp.zeros_like(out_ref)
    add_pairs(list_ref, 0, own_ref, target_ref, out_ref)


def own_pairs(rows, own):
    return pl.pallas_call(
        own_kernel,
        out_shape=(
            jax.ShapeDtypeStruct((NRHS, LEAVES * LEAF), jnp.float32),
            jax.ShapeDtypeStruct((2 * LIST,), jnp.int32),
        ),
        in_specs=[SM, ANY],
        out_specs=(VM, SM),
        scratch_shapes=[
            bf16(LEAVES + 1, ROWS, LEAF),
            bf16(LEAVES, LEAF, 128),
            pltpu.SemaphoreType.DMA((1,)),
        ],
        compiler_params=vmem(24),
        cost_estimate=cost(2 * 120 * 65536 * 272, 2 * MIB, 120 * 65536),
        name="own_pairs",
    )(rows, own)


def remote_kernel(
    list_ref, arrived_ref, left_ref, right_ref, own_hbm, field_ref, out_ref,
    table_ref, own_ref, target_ref, sem,
):
    near = fetch(
        sem,
        (own_hbm, own_ref),
        (field_ref, out_ref),
        (arrived_ref, table_ref.at[pl.ds(0, 2 * PEERS)]),
        (left_ref, table_ref.at[pl.ds(2 * PEERS, 2)]),
        (right_ref, table_ref.at[pl.ds(2 * PEERS + 2, 2)]),
    )
    table_ref[LOCAL] = jnp.zeros((ROWS, LEAF), jnp.bfloat16)
    near[0].wait()
    turn_targets(own_ref, target_ref)
    for copy in near[1:]:
        copy.wait()
    add_pairs(list_ref, LIST, table_ref, target_ref, out_ref)


def remote_pairs(lists, arrived, left, right, own, field):
    return pl.pallas_call(
        remote_kernel,
        out_shape=jax.ShapeDtypeStruct((NRHS, LEAVES * LEAF), jnp.float32),
        in_specs=[SM, ANY, ANY, ANY, ANY, ANY],
        out_specs=VM,
        scratch_shapes=[
            bf16(LOCAL + 1, ROWS, LEAF),
            bf16(LEAVES, ROWS, LEAF),
            bf16(LEAVES, LEAF, 128),
            pltpu.SemaphoreType.DMA((5,)),
        ],
        compiler_params=vmem(32),
        cost_estimate=cost(2 * 200 * 65536 * 272, 8 * MIB, 200 * 65536),
        name="remote_pairs",
    )(lists, arrived, left, right, own, field)


def turned(skel_ref, pair):
    return skel_ref[:, pl.ds(pair * 2 * RANK, 2 * RANK)].astype(jnp.float32).T


def field_pair(targets, blocks, halves):
    half_of = lax.broadcasted_iota(jnp.int32, (NRHS, 2 * RANK), 1) >> 6
    total = None
    for i, padded in enumerate((upper, below)):
        target = targets[i * RANK : (i + 1) * RANK]
        target_sq = jnp.sum(target * target, axis=1, keepdims=True) * 2
        source = jnp.concatenate([block[:DIM] for block in blocks[i]], axis=1)
        coeffs = jnp.concatenate(
            [
                jnp.where(half_of == half, block[DIM:], 0)
                for block, half in zip(blocks[i], halves[i], strict=True)
            ],
            axis=1,
        )
        wide = source.astype(jnp.float32)
        source_sq = jnp.sum(wide * wide, axis=0, keepdims=True) * 2
        power = dot((target * 4).astype(jnp.bfloat16), source) - target_sq - source_sq
        weights = jnp.exp(power).astype(jnp.bfloat16)
        term = dot(coeffs, padded(weights), NT)
        total = term if i == 0 else total + term
    return total


def far_one_kernel(far_ref, low_ref, arrived_ref, skel_hbm, out_ref, skel_ref, in_sem):
    (copy,) = fetch(in_sem, (skel_hbm, skel_ref))
    copy.wait()
    for pair in range(PAIRS):
        clusters = (2 * pair, 2 * pair + 1)
        blocks = [
            [arrived_ref[far_ref[c, j] >> 3, :ROWS, :] for j in range(FAR)] for c in clusters
        ]
        halves = [
            [
                ((far_ref[c, j] & 7) != low_ref[0, far_ref[c, j] >> 3]).astype(jnp.int32)
                for j in range(FAR)
            ]
            for c in clusters
        ]
        out_ref[pair] = field_pair(turned(skel_ref, pair), blocks, halves)


def far_one_field(far_one, low, arrived, skeleton_one):
    return pl.pallas_call(
        far_one_kernel,
        out_shape=jax.ShapeDtypeStruct((PAIRS, NRHS, 2 * RANK), jnp.float32),
        in_specs=[SM, SM, VM, ANY],
        out_specs=VM,
        scratch_shapes=[bf16(DIM, ONE * RANK), pltpu.SemaphoreType.DMA((1,))],
        compiler_params=vmem(16),
        cost_estimate=cost(1 << 28, 2 * MIB, 1 << 19),
        name="far_one_field",
    )(far_one, low, arrived, skeleton_one)


def final_kernel(
    far_ref, mine_ref, theirs_ref, field_one_ref, near_ref, skel_hbm, one_hbm, two_hbm, basis_hbm,
    out_ref, skel_ref, one_ref, two_ref, basis_ref, in_sem,
):
    core = lax.rem(lax.axis_index("leaf"), 2)
    skel_copy, two_copy, one_copy, basis_copy = fetch(
        in_sem, (skel_hbm, skel_ref), (two_hbm, two_ref), (one_hbm, one_ref), (basis_hbm, basis_ref)
    )

    def split(x):
        high = x.astype(jnp.bfloat16)
        return jnp.concatenate([high, (x - high.astype(jnp.float32)).astype(jnp.bfloat16)], axis=0)

    def exact(parts, b):
        both = dot(parts, b)
        return both[:NRHS] + both[NRHS:]

    def whole(e, j):
        b = far_ref[e, j]
        rows = jnp.where((b & 1) == core, mine_ref[b >> 1], theirs_ref[b >> 1]).astype(jnp.float32)
        return jnp.concatenate([rows, pltpu.roll(rows, RANK, 1)], axis=0).astype(jnp.bfloat16)

    blocks = [[whole(e, j) for j in range(FAR)] for e in range(TWO)]
    skel_copy.wait()
    field_two = split(field_pair(turned(skel_ref, 0), blocks, [[0] * FAR] * TWO))
    two_copy.wait()
    from_two = [
        exact(field_two, padded(two_ref[e])) for e, padded in enumerate((upper, below))
    ]
    one_copy.wait()
    down_leaf = []
    for pair in range(PAIRS):
        parent = from_two[pair // 2][:, (pair % 2) * 2 * RANK : (pair % 2 + 1) * 2 * RANK]
        down_one = split(field_one_ref[pair] + parent)
        for i, padded in enumerate((upper, below)):
            down_leaf.append(exact(down_one, padded(one_ref[2 * pair + i])).astype(jnp.bfloat16))
    basis_copy.wait()
    for leaf in range(LEAVES):
        columns = pl.ds(leaf * LEAF, LEAF)
        at = (leaf % 4) // 2
        half = down_leaf[leaf // 4][:, at * 2 * RANK : (at + 1) * 2 * RANK]
        basis = (upper, below)[leaf % 2](basis_ref[:, columns])
        out_ref[:, columns] = (near_ref[:, columns] + dot(half, basis)).astype(jnp.bfloat16)


def finish(far_two, mine, theirs, field_one, near, *arrays):
    return pl.pallas_call(
        final_kernel,
        out_shape=jax.ShapeDtypeStruct((NRHS, LEAVES * LEAF), jnp.bfloat16),
        in_specs=[SM] + [VM] * 4 + [ANY] * 4,
        out_specs=VM,
        scratch_shapes=[bf16(*a.shape) for a in arrays] + [pltpu.SemaphoreType.DMA((4,))],
        compiler_params=vmem(16),
        cost_estimate=cost(1 << 28, 3 * MIB, 1 << 17),
        name="finish",
    )(far_two, mine, theirs, field_one, near, *arrays)


def shift(x, step):
    return lax.ppermute(x, "leaf", [(i, (i + step) % PEERS) for i in range(PEERS)])


def swap(x):
    return lax.ppermute(x, "leaf", [(i, i ^ 1) for i in range(PEERS)])


def exchange(x):
    return lax.all_to_all(x, "leaf", split_axis=0, concat_axis=0, tiled=True)


def local(
    points, rhs, basis, transfer_one, transfer_two, skeleton_one, skeleton_two, near_source,
    far_one, far_two,
):
    me = lax.axis_index("leaf")
    wanted, low = ask(far_one)
    asked = exchange(wanted.reshape(PEERS, 1, PEERS)).reshape(PEERS, PEERS)
    message, to_right, to_left, own = pack(near_source, points, rhs)
    message, asked = lax.optimization_barrier((message, asked))
    arrived = exchange(message)
    columns = coefficients(rhs, basis, transfer_one, transfer_two, skeleton_one, skeleton_two)
    far_message = far_pack(asked[:, :2].reshape(-1), columns)
    field, lists = own_pairs(table_rows(near_source, me), own)
    to_right, to_left, far_message, field, lists = lax.optimization_barrier(
        (to_right, to_left, far_message, field, lists)
    )
    from_left, from_right = shift(to_right, 1), shift(to_left, -1)
    far_message, arrived, from_left, from_right = lax.optimization_barrier(
        (far_message, arrived, from_left, from_right)
    )
    far_arrived = exchange(far_message)
    near = remote_pairs(
        lists, arrived.reshape(2 * PEERS, ROWS, LEAF), from_left, from_right, own, field
    )
    far_arrived, near = lax.optimization_barrier((far_arrived, near))
    mine = far_arrived[:, ROWS:, :]
    theirs = swap(mine)
    field_one = far_one_field(far_one, low, far_arrived, skeleton_one)
    return finish(
        far_two, mine, theirs, field_one, near, skeleton_two, transfer_one, transfer_two, basis
    )


def solution(mesh):
    placed = (
        P(None, "leaf"),
        P(None, "leaf"),
        P(None, "leaf"),
        P("leaf", None, None),
        P("leaf", None, None),
        P(None, "leaf"),
        P(None, "leaf"),
        P(),
        P("leaf", None),
        P("leaf", None),
    )
    return jax.shard_map(
        local, mesh=mesh, in_specs=placed, out_specs=P(None, "leaf"), check_vma=False
    )
```

```python
import jax
import jax.numpy as jnp
from jax import lax
from jax.experimental import pallas as pl
from jax.experimental.pallas import tpu as pltpu
from jax.sharding import PartitionSpec as P

DIM = 32
NRHS = 16
RANK = 64
LEAF = 256
NEAR = 10
FAR = 8
LEAVES = 32
ONE = 8
TWO = 2
PAIRS = ONE // 2
ROWS = DIM + NRHS
PEERS = 128
LOCAL = 2 * PEERS + 4
TABLE = LOCAL + LEAVES
GROUP = 16
LIST = 384
STRIDE = 512
HALF_ROWS = ROWS // 2
MESSAGE = ROWS + HALF_ROWS
BLOCK = 2 * ROWS
ASK = 2 * BLOCK
NEAR_MESSAGE = ASK + 16
MIB = 1 << 20

NT = (((1,), (1,)), ((), ()))
NN = (((1,), (0,)), ((), ()))


def dot(a, b, dims=NN):
    return lax.dot_general(a, b, dims, preferred_element_type=jnp.float32)


def vmem(limit):
    return pltpu.CompilerParams(vmem_limit_bytes=limit * MIB)


def cost(flops, moved, exps=0):
    return pl.CostEstimate(flops=flops, bytes_accessed=moved, transcendentals=exps)


def fetch(sem, *pairs):
    copies = [pltpu.make_async_copy(a, b, sem.at[i]) for i, (a, b) in enumerate(pairs)]
    for copy in copies:
        copy.start()
    return copies


def bf16(*shape):
    return pltpu.VMEM(shape, jnp.bfloat16)


ANY = pl.BlockSpec(memory_space=pl.ANY)
VM = pl.BlockSpec(memory_space=pltpu.VMEM)
SM = pl.BlockSpec(memory_space=pltpu.SMEM)


def pack_kernel(
    source_ref, far_ref, points_ref, rhs_ref, msg_ref, right_ref, left_ref, own_ref, low_ref,
    lists_ref, points_vmem, rhs_vmem, block_ref, ask_ref, row_ref, row_smem,
    in_sem, row_sem, ask_sem, msg_sem, side_sem,
):
    me = lax.axis_index("leaf")
    listed = pltpu.make_async_copy(source_ref, lists_ref, row_sem)
    listed.start()
    filled = fetch(in_sem, (points_ref, points_vmem), (rhs_ref, rhs_vmem))
    peer = lax.broadcasted_iota(jnp.int32, (PEERS, FAR), 0) * ONE
    low = high = None
    for i in range(ONE):
        at = far_ref[i : i + 1, :] - peer
        inside = (at >> 3) == 0
        a, b = jnp.where(inside, at, ONE), jnp.where(inside, at, -1)
        low = a if i == 0 else jnp.minimum(low, a)
        high = b if i == 0 else jnp.maximum(high, b)
    low = jnp.min(low.astype(jnp.float32), axis=1, keepdims=True)
    high = jnp.max(high.astype(jnp.float32), axis=1, keepdims=True)
    lane = lax.broadcasted_iota(jnp.int32, (PEERS, PEERS), 1)
    wanted = jnp.where(lane < RANK, low, high)
    ask_ref[...] = jnp.broadcast_to(
        wanted[:, None, :], (PEERS, NEAR_MESSAGE - ASK, 2 * RANK)
    ).astype(jnp.bfloat16)
    asked = pltpu.make_async_copy(ask_ref, msg_ref.at[:, pl.ds(ASK, NEAR_MESSAGE - ASK)], ask_sem)
    asked.start()
    across = lax.broadcasted_iota(jnp.int32, (ONE, PEERS), 1) * ONE
    low = None
    for j in range(FAR):
        at = far_ref[:, j : j + 1] - across
        a = jnp.where((at >> 3) == 0, at, ONE)
        low = a if j == 0 else jnp.minimum(low, a)
    low = jnp.min(low.astype(jnp.float32), axis=0, keepdims=True)
    low_ref[...] = jnp.broadcast_to(low, (ONE, PEERS)).astype(jnp.int32)
    listed.wait()
    width = PEERS * LEAVES
    def marks(lists):
        mine = lists - me * LEAVES
        inside = (mine >> 5) == 0
        return (
            jnp.where(inside, mine, LEAVES),
            jnp.where(inside, -mine, 1),
            jnp.where(inside, 1 << (mine & 31), 0),
        )

    low, high, bits = marks(lists_ref[:8, :])
    for k in range(8, NEAR):
        a, b, c = (jnp.broadcast_to(v, (8, width)) for v in marks(lists_ref[k : k + 1, :]))
        low, high, bits = jnp.minimum(low, a), jnp.minimum(high, b), bits | c
    for step in (4, 2, 1):
        low = jnp.minimum(low, pltpu.roll(low, step, 0))
        high = jnp.minimum(high, pltpu.roll(high, step, 0))
        bits = bits | pltpu.roll(bits, step, 0)
    upper_rows = lax.broadcasted_iota(jnp.int32, (8, width), 0) < 4
    both = jnp.where(upper_rows, low, high)
    for step in (16, 8, 4, 2, 1):
        both = jnp.minimum(both, pltpu.roll(both, width - step, 1))
        bits = bits | pltpu.roll(bits, width - step, 1)
    low, high = both, -pltpu.roll(both, 4, 0)
    place = lax.broadcasted_iota(jnp.int32, (8, width), 1) & 31
    row_ref[...] = jnp.where(
        place == 0, low, jnp.where(place == 1, pltpu.roll(high, 1, 1), pltpu.roll(bits, 2, 1))
    )
    copy = pltpu.make_async_copy(row_ref.at[0:1], row_smem, row_sem)
    copy.start()
    for fill in filled:
        fill.wait()
    for leaf in range(LEAVES):
        for half in range(2):
            columns = pl.ds(leaf * LEAF + half * 128, 128)
            block_ref[leaf, pl.ds(half * ROWS, DIM), :] = points_vmem[:, columns]
            block_ref[leaf, pl.ds(half * ROWS + DIM, NRHS), :] = rhs_vmem[:, columns]
    own = pltpu.make_async_copy(block_ref, own_ref, in_sem.at[0])
    own.start()
    copy.wait()

    def send(peer, _):
        for slot in range(2):
            leaf = row_smem[0, peer * LEAVES + slot] & 31
            pltpu.make_async_copy(
                block_ref.at[leaf], msg_ref.at[peer, pl.ds(slot * BLOCK, BLOCK)], msg_sem
            ).start()
        return 0

    lax.fori_loop(0, PEERS, send, 0, unroll=8)
    for side, (ref, step) in enumerate(((right_ref, 1), (left_ref, PEERS - 1))):
        at = lax.rem(me + step, PEERS) * LEAVES
        between = row_smem[0, at + 2]
        between = between & ~(1 << (row_smem[0, at] & 31)) & ~(1 << (row_smem[0, at + 1] & 31))

        def scan(bit, found):
            has = ((between >> bit) & 1) == 1
            return jnp.where(has & (found[0] < 0), bit, found[0]), jnp.where(has, bit, found[1])

        first, last = lax.fori_loop(0, LEAVES, scan, (jnp.int32(-1), jnp.int32(0)))
        for slot, leaf in enumerate((first & 31, last & 31)):
            pltpu.make_async_copy(block_ref.at[leaf], ref.at[slot], side_sem.at[side]).start()
    sent = msg_ref.at[:, pl.ds(0, ASK)]
    pltpu.make_async_copy(sent, sent, msg_sem).wait()
    asked.wait()
    for side, ref in enumerate((right_ref, left_ref)):
        pltpu.make_async_copy(ref, ref, side_sem.at[side]).wait()
    own.wait()


def pack(source, far_one, points, rhs):
    block = jax.ShapeDtypeStruct((LEAVES, BLOCK, 128), jnp.bfloat16)
    side = jax.ShapeDtypeStruct((2, BLOCK, 128), jnp.bfloat16)
    return pl.pallas_call(
        pack_kernel,
        out_shape=(
            jax.ShapeDtypeStruct((PEERS, NEAR_MESSAGE, 128), jnp.bfloat16), side, side, block,
            jax.ShapeDtypeStruct((ONE, PEERS), jnp.int32),
        ),
        in_specs=[ANY, VM, ANY, ANY],
        out_specs=(ANY, ANY, ANY, ANY, VM),
        scratch_shapes=[
            pltpu.VMEM((NEAR, PEERS * LEAVES), jnp.int32),
            bf16(*points.shape),
            bf16(*rhs.shape),
            bf16(LEAVES, BLOCK, 128),
            bf16(PEERS, NEAR_MESSAGE - ASK, 2 * RANK),
            pltpu.VMEM((8, PEERS * LEAVES), jnp.int32),
            pltpu.SMEM((1, PEERS * LEAVES), jnp.int32),
            pltpu.SemaphoreType.DMA((2,)),
            pltpu.SemaphoreType.DMA,
            pltpu.SemaphoreType.DMA,
            pltpu.SemaphoreType.DMA,
            pltpu.SemaphoreType.DMA((2,)),
        ],
        compiler_params=vmem(56),
        cost_estimate=cost(1 << 20, 14 * MIB),
        name="pack",
    )(source.T, far_one, points, rhs)


def upper(b):
    return jnp.concatenate([b, jnp.zeros_like(b)], axis=0)


def below(b):
    return jnp.concatenate([jnp.zeros_like(b), b], axis=0)


def coeff_kernel(
    rhs_hbm, basis_hbm, one_hbm, two_hbm, skel_one_hbm, skel_two_hbm, out_ref,
    rhs_ref, basis_ref, one_ref, two_ref, skel_one_ref, skel_two_ref, sem,
):
    for copy in fetch(
        sem, (rhs_hbm, rhs_ref), (basis_hbm, basis_ref), (one_hbm, one_ref), (two_hbm, two_ref),
        (skel_one_hbm, skel_one_ref), (skel_two_hbm, skel_two_ref),
    ):
        copy.wait()

    def leaf_pair(leaf):
        a, b = (pl.ds((leaf + i) * LEAF, LEAF) for i in range(2))
        return (
            dot(rhs_ref[:, a], upper(basis_ref[:, a]), NT)
            + dot(rhs_ref[:, b], below(basis_ref[:, b]), NT)
        ).astype(jnp.bfloat16)

    def lift_pair(children, transfer_ref, cluster):
        return (
            dot(children[0], upper(transfer_ref[cluster]), NT)
            + dot(children[1], below(transfer_ref[cluster + 1]), NT)
        ).astype(jnp.bfloat16)

    pairs = []
    for pair in range(PAIRS):
        joined = [
            jnp.concatenate([leaf_pair(4 * c), leaf_pair(4 * c + 2)], axis=1)
            for c in (2 * pair, 2 * pair + 1)
        ]
        pairs.append(lift_pair(joined, one_ref, 2 * pair))
        out_ref[pair, :DIM, :] = skel_one_ref[:, pl.ds(pair * 2 * RANK, 2 * RANK)]
        out_ref[pair, DIM:, :] = pairs[-1]
    joined = [jnp.concatenate(pairs[2 * e : 2 * e + 2], axis=1) for e in range(TWO)]
    out_ref[PAIRS, :DIM, :] = skel_two_ref[...]
    out_ref[PAIRS, DIM:, :] = lift_pair(joined, two_ref, 0)


def coefficients(*args):
    return pl.pallas_call(
        coeff_kernel,
        out_shape=jax.ShapeDtypeStruct((PAIRS + 1, ROWS, 2 * RANK), jnp.bfloat16),
        in_specs=[ANY] * 6,
        out_specs=VM,
        scratch_shapes=[bf16(*a.shape) for a in args] + [pltpu.SemaphoreType.DMA((6,))],
        compiler_params=vmem(24),
        cost_estimate=cost(1 << 26, 2 * MIB),
        name="coefficients",
    )(*args)


def far_pack_kernel(
    arrived_ref, columns_ref, out_hbm, out_ref, ask_ref, cluster_ref, sem, out_sem
):
    (copy,) = fetch(sem, (arrived_ref.at[:, pl.ds(ASK, NEAR_MESSAGE - ASK)], ask_ref))
    left = lax.broadcasted_iota(jnp.int32, (ROWS, 2 * RANK), 1) < RANK
    for pair in range(PAIRS):
        wide = columns_ref[pair].astype(jnp.float32)
        turned = pltpu.roll(wide, RANK, 1)
        cluster_ref[2 * pair] = jnp.where(left, wide, turned)
        cluster_ref[2 * pair + 1] = jnp.where(left, turned, wide)
    wide = columns_ref[PAIRS].astype(jnp.float32)
    turned = pltpu.roll(wide, RANK, 1)
    half = left[:HALF_ROWS]
    second = (
        jnp.where(half, wide[:HALF_ROWS], turned[HALF_ROWS:]),
        jnp.where(half, turned[:HALF_ROWS], wide[HALF_ROWS:]),
    )
    copy.wait()

    def fill(chip, _):
        for core in range(2):
            peer = 2 * chip + core
            wanted = ask_ref[peer].astype(jnp.float32)[:8]
            wanted = jnp.concatenate([wanted] * (ROWS // 8), axis=0)
            first = cluster_ref[0]
            for c in range(1, ONE):
                first = jnp.where(wanted == c, cluster_ref[c], first)
            out_ref[peer] = jnp.concatenate([first, second[core]], axis=0).astype(jnp.bfloat16)
        return 0

    sent = []
    for part in range(4):
        lax.fori_loop(part * PEERS // 8, (part + 1) * PEERS // 8, fill, 0, unroll=4)
        peers = pl.ds(part * PEERS // 4, PEERS // 4)
        sent.append(pltpu.make_async_copy(out_ref.at[peers], out_hbm.at[peers], out_sem.at[part]))
        sent[-1].start()
    for copy in sent:
        copy.wait()


def far_pack(arrived, columns):
    return pl.pallas_call(
        far_pack_kernel,
        out_shape=jax.ShapeDtypeStruct((PEERS, MESSAGE, 2 * RANK), jnp.bfloat16),
        in_specs=[ANY, VM],
        out_specs=ANY,
        scratch_shapes=[
            bf16(PEERS, MESSAGE, 2 * RANK),
            bf16(PEERS, NEAR_MESSAGE - ASK, 2 * RANK),
            pltpu.VMEM((ONE, ROWS, 2 * RANK), jnp.float32),
            pltpu.SemaphoreType.DMA((1,)),
            pltpu.SemaphoreType.DMA((4,)),
        ],
        compiler_params=vmem(56),
        cost_estimate=cost(1 << 20, 5 * MIB),
        name="far_pack",
    )(arrived, columns)


def table_rows(near_source, me):
    mine = lax.dynamic_slice_in_dim(near_source, me * LEAVES, LEAVES, 0).reshape(-1)
    device, leaf = mine >> 5, mine & 31
    from_peer = device[:, None] == jnp.arange(PEERS, dtype=jnp.int32)[None, :]
    low = jnp.min(jnp.where(from_peer, leaf[:, None], LEAVES), axis=0)
    high = jnp.max(jnp.where(from_peer, leaf[:, None], -1), axis=0)
    low_of = jnp.sum(jnp.where(from_peer, low[None, :], 0), axis=1)
    high_of = jnp.sum(jnp.where(from_peer, high[None, :], 0), axis=1)
    row = device + PEERS * (leaf != low_of)
    inner = (leaf > low_of) & (leaf < high_of)
    for side, step in enumerate((PEERS - 1, 1)):
        chosen = inner & (device == (me + step) % PEERS)
        first = jnp.min(jnp.where(chosen, leaf, LEAVES))
        row = jnp.where(chosen, 2 * PEERS + 2 * side + (leaf != first), row)
    return jnp.where(device == me, LOCAL + leaf, row)


def with_square(block, first):
    wide = block.astype(jnp.float32)
    square = jnp.sum(wide * wide, axis=0, keepdims=True) * -2
    high = square.astype(jnp.bfloat16).astype(jnp.float32)
    middle = (square - high).astype(jnp.bfloat16).astype(jnp.float32)
    low = square - high - middle
    at = lax.broadcasted_iota(jnp.int32, (16, LEAF), 0)
    ones, parts = (3, 0) if first else (0, 3)
    extra = jnp.where((at >= ones) & (at < ones + 3), 1.0, 0.0)
    for i, part in enumerate((high, middle, low)):
        extra = jnp.where(at == parts + i, part, extra)
    if first:
        return jnp.concatenate([wide * 4, extra], axis=0).T.astype(jnp.bfloat16)
    return jnp.concatenate([block, extra.astype(jnp.bfloat16)], axis=0)


def points_of(block):
    return jnp.concatenate([block[:DIM], block[ROWS : ROWS + DIM]], axis=1)


def rhs_of(block):
    return jnp.concatenate([block[DIM:ROWS], block[ROWS + DIM :]], axis=1)


def turn_targets(own_ref, target_ref):
    def turn(leaf, _):
        target_ref[leaf, :, :ROWS] = with_square(points_of(own_ref[leaf]), True)
        return 0

    lax.fori_loop(0, LEAVES, turn, 0, unroll=2)


def add_pairs(list_ref, start, table_ref, target_ref, out_ref):
    def step(i, _):
        pairs = []
        for u in range(GROUP):
            pair = list_ref[start + i * GROUP + u]
            target, row = pair // STRIDE, pair & (STRIDE - 1)
            weights = jnp.exp(
                dot(target_ref[target, :, :ROWS], with_square(points_of(table_ref[row]), False))
            ).astype(jnp.bfloat16)
            pairs.append((target, row, weights))
        terms = [(t, dot(rhs_of(table_ref[row]), weights, NT)) for t, row, weights in pairs]
        for target, term in terms:
            columns = pl.ds(pl.multiple_of(target * LEAF, LEAF), LEAF)
            out_ref[:, columns] += term
        return 0

    lax.fori_loop(0, (list_ref[start + LIST - 1] + GROUP - 1) // GROUP, step, 0)


def own_kernel(row_ref, own_hbm, out_ref, list_ref, own_ref, target_ref, sem):
    (copy,) = fetch(sem, (own_hbm, own_ref.at[pl.ds(0, LEAVES)]))

    def sort(target, counts):
        mine, others = counts
        for k in range(NEAR):
            row = row_ref[target * NEAR + k]
            list_ref[mine] = target * STRIDE + jnp.maximum(row - LOCAL, 0)
            list_ref[LIST + others] = target * STRIDE + row
            is_mine = (row >= LOCAL).astype(jnp.int32)
            mine, others = mine + is_mine, others + 1 - is_mine
        return mine, others

    mine, others = lax.fori_loop(0, LEAVES, sort, (jnp.int32(0), jnp.int32(0)))
    for u in range(GROUP):
        list_ref[mine + u] = LEAVES
        list_ref[LIST + others + u] = LOCAL
    list_ref[LIST - 1] = mine
    list_ref[2 * LIST - 1] = others
    own_ref[LEAVES] = jnp.zeros((BLOCK, 128), jnp.bfloat16)
    copy.wait()
    turn_targets(own_ref, target_ref)
    out_ref[...] = jnp.zeros_like(out_ref)
    add_pairs(list_ref, 0, own_ref, target_ref, out_ref)


def own_pairs(rows, own):
    return pl.pallas_call(
        own_kernel,
        out_shape=(
            jax.ShapeDtypeStruct((NRHS, LEAVES * LEAF), jnp.float32),
            jax.ShapeDtypeStruct((2 * LIST,), jnp.int32),
        ),
        in_specs=[SM, ANY],
        out_specs=(VM, SM),
        scratch_shapes=[
            bf16(LEAVES + 1, BLOCK, 128),
            bf16(LEAVES, LEAF, 128),
            pltpu.SemaphoreType.DMA((1,)),
        ],
        compiler_params=vmem(24),
        cost_estimate=cost(2 * 120 * 65536 * 272, 2 * MIB, 120 * 65536),
        name="own_pairs",
    )(rows, own)


def remote_kernel(
    list_ref, arrived_ref, left_ref, right_ref, own_hbm, field_ref, out_ref,
    table_ref, own_ref, target_ref, sem,
):
    near = fetch(
        sem,
        (own_hbm, own_ref),
        (field_ref, out_ref),
        (arrived_ref.at[:, pl.ds(0, BLOCK)], table_ref.at[pl.ds(0, PEERS)]),
        (arrived_ref.at[:, pl.ds(BLOCK, BLOCK)], table_ref.at[pl.ds(PEERS, PEERS)]),
        (left_ref, table_ref.at[pl.ds(2 * PEERS, 2)]),
        (right_ref, table_ref.at[pl.ds(2 * PEERS + 2, 2)]),
    )
    table_ref[LOCAL] = jnp.zeros((BLOCK, 128), jnp.bfloat16)
    near[0].wait()
    turn_targets(own_ref, target_ref)
    for copy in near[1:]:
        copy.wait()
    add_pairs(list_ref, LIST, table_ref, target_ref, out_ref)


def remote_pairs(lists, arrived, left, right, own, field):
    return pl.pallas_call(
        remote_kernel,
        out_shape=jax.ShapeDtypeStruct((NRHS, LEAVES * LEAF), jnp.float32),
        in_specs=[SM, ANY, ANY, ANY, ANY, ANY],
        out_specs=VM,
        scratch_shapes=[
            bf16(LOCAL + 1, BLOCK, 128),
            bf16(LEAVES, BLOCK, 128),
            bf16(LEAVES, LEAF, 128),
            pltpu.SemaphoreType.DMA((6,)),
        ],
        compiler_params=vmem(32),
        cost_estimate=cost(2 * 200 * 65536 * 272, 8 * MIB, 200 * 65536),
        name="remote_pairs",
    )(lists, arrived, left, right, own, field)


def turned(skel_ref, pair):
    return skel_ref[:, pl.ds(pair * 2 * RANK, 2 * RANK)].astype(jnp.float32).T


def field_pair(targets, blocks, halves):
    half_of = lax.broadcasted_iota(jnp.int32, (NRHS, 2 * RANK), 1) >> 6
    total = None
    for i, padded in enumerate((upper, below)):
        target = targets[i * RANK : (i + 1) * RANK]
        target_sq = jnp.sum(target * target, axis=1, keepdims=True) * 2
        source = jnp.concatenate([block[:DIM] for block in blocks[i]], axis=1)
        coeffs = jnp.concatenate(
            [
                jnp.where(half_of == half, block[DIM:], 0)
                for block, half in zip(blocks[i], halves[i], strict=True)
            ],
            axis=1,
        )
        wide = source.astype(jnp.float32)
        source_sq = jnp.sum(wide * wide, axis=0, keepdims=True) * 2
        power = dot((target * 4).astype(jnp.bfloat16), source) - target_sq - source_sq
        weights = jnp.exp(power).astype(jnp.bfloat16)
        term = dot(coeffs, padded(weights), NT)
        total = term if i == 0 else total + term
    return total


def far_one_kernel(
    far_ref, low_ref, arrived_ref, skel_hbm, near_hbm, one_hbm, out_ref, near_ref, one_ref, skel_ref,
    in_sem,
):
    copy, *brought = fetch(in_sem, (skel_hbm, skel_ref), (near_hbm, near_ref), (one_hbm, one_ref))
    copy.wait()
    for pair in range(PAIRS):
        clusters = (2 * pair, 2 * pair + 1)
        blocks = [
            [arrived_ref[far_ref[c, j] >> 3, :ROWS, :] for j in range(FAR)] for c in clusters
        ]
        halves = [
            [
                ((far_ref[c, j] & 7) != low_ref[0, far_ref[c, j] >> 3]).astype(jnp.int32)
                for j in range(FAR)
            ]
            for c in clusters
        ]
        out_ref[pair] = field_pair(turned(skel_ref, pair), blocks, halves)
    for copy in brought:
        copy.wait()


def far_one_field(far_one, low, arrived, skeleton_one, near, transfer_one):
    return pl.pallas_call(
        far_one_kernel,
        out_shape=(
            jax.ShapeDtypeStruct((PAIRS, NRHS, 2 * RANK), jnp.float32),
            jax.ShapeDtypeStruct(near.shape, near.dtype),
            jax.ShapeDtypeStruct(transfer_one.shape, transfer_one.dtype),
        ),
        in_specs=[SM, SM, VM, ANY, ANY, ANY],
        out_specs=(VM, VM, VM),
        scratch_shapes=[bf16(DIM, ONE * RANK), pltpu.SemaphoreType.DMA((3,))],
        compiler_params=vmem(16),
        cost_estimate=cost(1 << 28, 2 * MIB, 1 << 19),
        name="far_one_field",
    )(far_one, low, arrived, skeleton_one, near, transfer_one)


def final_kernel(
    far_ref, mine_ref, theirs_ref, field_one_ref, near_ref, one_ref, skel_hbm, two_hbm, basis_hbm,
    out_ref, skel_ref, two_ref, basis_ref, in_sem,
):
    core = lax.rem(lax.axis_index("leaf"), 2)
    skel_copy, two_copy, basis_copy = fetch(
        in_sem, (skel_hbm, skel_ref), (two_hbm, two_ref), (basis_hbm, basis_ref)
    )

    def split(x):
        high = x.astype(jnp.bfloat16)
        return jnp.concatenate([high, (x - high.astype(jnp.float32)).astype(jnp.bfloat16)], axis=0)

    def exact(parts, b):
        both = dot(parts, b)
        return both[:NRHS] + both[NRHS:]

    def whole(e, j):
        b = far_ref[e, j]
        rows = jnp.where((b & 1) == core, mine_ref[b >> 1], theirs_ref[b >> 1]).astype(jnp.float32)
        return jnp.concatenate([rows, pltpu.roll(rows, RANK, 1)], axis=0).astype(jnp.bfloat16)

    blocks = [[whole(e, j) for j in range(FAR)] for e in range(TWO)]
    skel_copy.wait()
    field_two = split(field_pair(turned(skel_ref, 0), blocks, [[0] * FAR] * TWO))
    two_copy.wait()
    from_two = [
        exact(field_two, padded(two_ref[e])) for e, padded in enumerate((upper, below))
    ]
    down_leaf = []
    for pair in range(PAIRS):
        parent = from_two[pair // 2][:, (pair % 2) * 2 * RANK : (pair % 2 + 1) * 2 * RANK]
        down_one = split(field_one_ref[pair] + parent)
        for i, padded in enumerate((upper, below)):
            down_leaf.append(exact(down_one, padded(one_ref[2 * pair + i])).astype(jnp.bfloat16))
    basis_copy.wait()
    for leaf in range(LEAVES):
        columns = pl.ds(leaf * LEAF, LEAF)
        at = (leaf % 4) // 2
        half = down_leaf[leaf // 4][:, at * 2 * RANK : (at + 1) * 2 * RANK]
        basis = (upper, below)[leaf % 2](basis_ref[:, columns])
        out_ref[:, columns] = (near_ref[:, columns] + dot(half, basis)).astype(jnp.bfloat16)


def finish(far_two, mine, theirs, field_one, near, transfer_one, *arrays):
    return pl.pallas_call(
        final_kernel,
        out_shape=jax.ShapeDtypeStruct((NRHS, LEAVES * LEAF), jnp.bfloat16),
        in_specs=[SM] + [VM] * 5 + [ANY] * 3,
        out_specs=VM,
        scratch_shapes=[bf16(*a.shape) for a in arrays] + [pltpu.SemaphoreType.DMA((3,))],
        compiler_params=vmem(16),
        cost_estimate=cost(1 << 28, 3 * MIB, 1 << 17),
        name="finish",
    )(far_two, mine, theirs, field_one, near, transfer_one, *arrays)


def shift(x, step):
    return lax.ppermute(x, "leaf", [(i, (i + step) % PEERS) for i in range(PEERS)])


def swap(x):
    return lax.ppermute(x, "leaf", [(i, i ^ 1) for i in range(PEERS)])


def exchange(x):
    return lax.all_to_all(x, "leaf", split_axis=0, concat_axis=0, tiled=True)


def local(
    points, rhs, basis, transfer_one, transfer_two, skeleton_one, skeleton_two, near_source,
    far_one, far_two,
):
    me = lax.axis_index("leaf")
    message, to_right, to_left, own, low = pack(near_source, far_one, points, rhs)
    arrived = exchange(message)
    columns = coefficients(rhs, basis, transfer_one, transfer_two, skeleton_one, skeleton_two)
    field, lists = own_pairs(table_rows(near_source, me), own)
    to_right, to_left, columns, field, lists = lax.optimization_barrier(
        (to_right, to_left, columns, field, lists)
    )
    from_left, from_right = shift(to_right, 1), shift(to_left, -1)
    arrived, from_left, from_right = lax.optimization_barrier((arrived, from_left, from_right))
    far_arrived = exchange(far_pack(arrived, columns))
    near = remote_pairs(lists, arrived, from_left, from_right, own, field)
    far_arrived, near = lax.optimization_barrier((far_arrived, near))
    mine = far_arrived[:, ROWS:, :]
    theirs = swap(mine)
    field_one, near, transfer_one = far_one_field(
        far_one, low, far_arrived, skeleton_one, near, transfer_one
    )
    return finish(
        far_two, mine, theirs, field_one, near, transfer_one, skeleton_two, transfer_two, basis
    )


def solution(mesh):
    placed = (
        P(None, "leaf"),
        P(None, "leaf"),
        P(None, "leaf"),
        P("leaf", None, None),
        P("leaf", None, None),
        P(None, "leaf"),
        P(None, "leaf"),
        P(),
        P("leaf", None),
        P("leaf", None),
    )
    return jax.shard_map(
        local, mesh=mesh, in_specs=placed, out_specs=P(None, "leaf"), check_vma=False
    )
```

```python
import jax
import jax.numpy as jnp
from jax import lax
from jax.experimental import pallas as pl
from jax.experimental.pallas import tpu as pltpu
from jax.sharding import PartitionSpec as P

DIM = 32
NRHS = 16
RANK = 64
LEAF = 256
NEAR = 10
FAR = 8
LEAVES = 32
ONE = 8
TWO = 2
PAIRS = ONE // 2
ROWS = DIM + NRHS
PEERS = 128
LOCAL = 2 * PEERS + 4
TABLE = LOCAL + LEAVES
GROUP = 16
LIST = 384
STRIDE = 512
HALF_ROWS = ROWS // 2
MESSAGE = ROWS + HALF_ROWS
BLOCK = 2 * ROWS
ASK = 2 * BLOCK
NEAR_MESSAGE = ASK + 16
MIB = 1 << 20

NT = (((1,), (1,)), ((), ()))
NN = (((1,), (0,)), ((), ()))


def dot(a, b, dims=NN):
    return lax.dot_general(a, b, dims, preferred_element_type=jnp.float32)


def vmem(limit):
    return pltpu.CompilerParams(vmem_limit_bytes=limit * MIB)


def cost(flops, moved, exps=0):
    return pl.CostEstimate(flops=flops, bytes_accessed=moved, transcendentals=exps)


def fetch(sem, *pairs):
    copies = [pltpu.make_async_copy(a, b, sem.at[i]) for i, (a, b) in enumerate(pairs)]
    for copy in copies:
        copy.start()
    return copies


def bf16(*shape):
    return pltpu.VMEM(shape, jnp.bfloat16)


ANY = pl.BlockSpec(memory_space=pl.ANY)
VM = pl.BlockSpec(memory_space=pltpu.VMEM)
SM = pl.BlockSpec(memory_space=pltpu.SMEM)


def pack_kernel(
    source_ref, far_ref, points_ref, rhs_ref, msg_ref, right_ref, left_ref, own_ref, low_ref,
    lists_ref, points_vmem, rhs_vmem, block_ref, ask_ref, row_ref, row_smem,
    in_sem, row_sem, ask_sem, msg_sem, side_sem,
):
    me = lax.axis_index("leaf")
    listed = pltpu.make_async_copy(source_ref, lists_ref, row_sem)
    listed.start()
    filled = fetch(in_sem, (points_ref, points_vmem), (rhs_ref, rhs_vmem))
    peer = lax.broadcasted_iota(jnp.int32, (PEERS, FAR), 0) * ONE
    low = high = None
    for i in range(ONE):
        at = far_ref[i : i + 1, :] - peer
        inside = (at >> 3) == 0
        a, b = jnp.where(inside, at, ONE), jnp.where(inside, at, -1)
        low = a if i == 0 else jnp.minimum(low, a)
        high = b if i == 0 else jnp.maximum(high, b)
    low = jnp.min(low.astype(jnp.float32), axis=1, keepdims=True)
    high = jnp.max(high.astype(jnp.float32), axis=1, keepdims=True)
    lane = lax.broadcasted_iota(jnp.int32, (PEERS, PEERS), 1)
    wanted = jnp.where(lane < RANK, low, high)
    ask_ref[...] = jnp.broadcast_to(
        wanted[:, None, :], (PEERS, NEAR_MESSAGE - ASK, 2 * RANK)
    ).astype(jnp.bfloat16)
    asked = pltpu.make_async_copy(ask_ref, msg_ref.at[:, pl.ds(ASK, NEAR_MESSAGE - ASK)], ask_sem)
    asked.start()
    across = lax.broadcasted_iota(jnp.int32, (ONE, PEERS), 1) * ONE
    low = None
    for j in range(FAR):
        at = far_ref[:, j : j + 1] - across
        a = jnp.where((at >> 3) == 0, at, ONE)
        low = a if j == 0 else jnp.minimum(low, a)
    low = jnp.min(low.astype(jnp.float32), axis=0, keepdims=True)
    low_ref[...] = jnp.broadcast_to(low, (ONE, PEERS)).astype(jnp.int32)
    listed.wait()
    width = PEERS * LEAVES
    def marks(lists):
        mine = lists - me * LEAVES
        inside = (mine >> 5) == 0
        return (
            jnp.where(inside, mine, LEAVES),
            jnp.where(inside, -mine, 1),
            jnp.where(inside, 1 << (mine & 31), 0),
        )

    low, high, bits = marks(lists_ref[:8, :])
    for k in range(8, NEAR):
        a, b, c = (jnp.broadcast_to(v, (8, width)) for v in marks(lists_ref[k : k + 1, :]))
        low, high, bits = jnp.minimum(low, a), jnp.minimum(high, b), bits | c
    for step in (4, 2, 1):
        low = jnp.minimum(low, pltpu.roll(low, step, 0))
        high = jnp.minimum(high, pltpu.roll(high, step, 0))
        bits = bits | pltpu.roll(bits, step, 0)
    upper_rows = lax.broadcasted_iota(jnp.int32, (8, width), 0) < 4
    both = jnp.where(upper_rows, low, high)
    for step in (16, 8, 4, 2, 1):
        both = jnp.minimum(both, pltpu.roll(both, width - step, 1))
        bits = bits | pltpu.roll(bits, width - step, 1)
    low, high = both, -pltpu.roll(both, 4, 0)
    place = lax.broadcasted_iota(jnp.int32, (8, width), 1) & 31
    row_ref[...] = jnp.where(
        place == 0, low, jnp.where(place == 1, pltpu.roll(high, 1, 1), pltpu.roll(bits, 2, 1))
    )
    copy = pltpu.make_async_copy(row_ref.at[0:1], row_smem, row_sem)
    copy.start()
    for fill in filled:
        fill.wait()
    for leaf in range(LEAVES):
        for half in range(2):
            columns = pl.ds(leaf * LEAF + half * 128, 128)
            block_ref[leaf, pl.ds(half * ROWS, DIM), :] = points_vmem[:, columns]
            block_ref[leaf, pl.ds(half * ROWS + DIM, NRHS), :] = rhs_vmem[:, columns]
    own = pltpu.make_async_copy(block_ref, own_ref, in_sem.at[0])
    own.start()
    copy.wait()

    def send(peer, _):
        for slot in range(2):
            leaf = row_smem[0, peer * LEAVES + slot] & 31
            pltpu.make_async_copy(
                block_ref.at[leaf], msg_ref.at[peer, pl.ds(slot * BLOCK, BLOCK)], msg_sem
            ).start()
        return 0

    lax.fori_loop(0, PEERS, send, 0, unroll=8)
    for side, (ref, step) in enumerate(((right_ref, 1), (left_ref, PEERS - 1))):
        at = lax.rem(me + step, PEERS) * LEAVES
        between = row_smem[0, at + 2]
        between = between & ~(1 << (row_smem[0, at] & 31)) & ~(1 << (row_smem[0, at + 1] & 31))

        def scan(bit, found):
            has = ((between >> bit) & 1) == 1
            return jnp.where(has & (found[0] < 0), bit, found[0]), jnp.where(has, bit, found[1])

        first, last = lax.fori_loop(0, LEAVES, scan, (jnp.int32(-1), jnp.int32(0)))
        for slot, leaf in enumerate((first & 31, last & 31)):
            pltpu.make_async_copy(block_ref.at[leaf], ref.at[slot], side_sem.at[side]).start()
    sent = msg_ref.at[:, pl.ds(0, ASK)]
    pltpu.make_async_copy(sent, sent, msg_sem).wait()
    asked.wait()
    for side, ref in enumerate((right_ref, left_ref)):
        pltpu.make_async_copy(ref, ref, side_sem.at[side]).wait()
    own.wait()


def pack(source, far_one, points, rhs):
    block = jax.ShapeDtypeStruct((LEAVES, BLOCK, 128), jnp.bfloat16)
    side = jax.ShapeDtypeStruct((2, BLOCK, 128), jnp.bfloat16)
    return pl.pallas_call(
        pack_kernel,
        out_shape=(
            jax.ShapeDtypeStruct((PEERS, NEAR_MESSAGE, 128), jnp.bfloat16), side, side, block,
            jax.ShapeDtypeStruct((ONE, PEERS), jnp.int32),
        ),
        in_specs=[ANY, VM, ANY, ANY],
        out_specs=(ANY, ANY, ANY, ANY, VM),
        scratch_shapes=[
            pltpu.VMEM((NEAR, PEERS * LEAVES), jnp.int32),
            bf16(*points.shape),
            bf16(*rhs.shape),
            bf16(LEAVES, BLOCK, 128),
            bf16(PEERS, NEAR_MESSAGE - ASK, 2 * RANK),
            pltpu.VMEM((8, PEERS * LEAVES), jnp.int32),
            pltpu.SMEM((1, PEERS * LEAVES), jnp.int32),
            pltpu.SemaphoreType.DMA((2,)),
            pltpu.SemaphoreType.DMA,
            pltpu.SemaphoreType.DMA,
            pltpu.SemaphoreType.DMA,
            pltpu.SemaphoreType.DMA((2,)),
        ],
        compiler_params=vmem(56),
        cost_estimate=cost(1 << 20, 14 * MIB),
        name="pack",
    )(source.T, far_one, points, rhs)


def upper(b):
    return jnp.concatenate([b, jnp.zeros_like(b)], axis=0)


def below(b):
    return jnp.concatenate([jnp.zeros_like(b), b], axis=0)


def coeff_kernel(
    rhs_hbm, basis_hbm, one_hbm, two_hbm, skel_one_hbm, skel_two_hbm, out_ref,
    rhs_ref, basis_ref, one_ref, two_ref, skel_one_ref, skel_two_ref, sem,
):
    for copy in fetch(
        sem, (rhs_hbm, rhs_ref), (basis_hbm, basis_ref), (one_hbm, one_ref), (two_hbm, two_ref),
        (skel_one_hbm, skel_one_ref), (skel_two_hbm, skel_two_ref),
    ):
        copy.wait()

    def leaf_pair(leaf):
        a, b = (pl.ds((leaf + i) * LEAF, LEAF) for i in range(2))
        return (
            dot(rhs_ref[:, a], upper(basis_ref[:, a]), NT)
            + dot(rhs_ref[:, b], below(basis_ref[:, b]), NT)
        ).astype(jnp.bfloat16)

    def lift_pair(children, transfer_ref, cluster):
        return (
            dot(children[0], upper(transfer_ref[cluster]), NT)
            + dot(children[1], below(transfer_ref[cluster + 1]), NT)
        ).astype(jnp.bfloat16)

    pairs = []
    for pair in range(PAIRS):
        joined = [
            jnp.concatenate([leaf_pair(4 * c), leaf_pair(4 * c + 2)], axis=1)
            for c in (2 * pair, 2 * pair + 1)
        ]
        pairs.append(lift_pair(joined, one_ref, 2 * pair))
        out_ref[pair, :DIM, :] = skel_one_ref[:, pl.ds(pair * 2 * RANK, 2 * RANK)]
        out_ref[pair, DIM:, :] = pairs[-1]
    joined = [jnp.concatenate(pairs[2 * e : 2 * e + 2], axis=1) for e in range(TWO)]
    out_ref[PAIRS, :DIM, :] = skel_two_ref[...]
    out_ref[PAIRS, DIM:, :] = lift_pair(joined, two_ref, 0)


def coefficients(*args):
    return pl.pallas_call(
        coeff_kernel,
        out_shape=jax.ShapeDtypeStruct((PAIRS + 1, ROWS, 2 * RANK), jnp.bfloat16),
        in_specs=[ANY] * 6,
        out_specs=VM,
        scratch_shapes=[bf16(*a.shape) for a in args] + [pltpu.SemaphoreType.DMA((6,))],
        compiler_params=vmem(24),
        cost_estimate=cost(1 << 26, 2 * MIB),
        name="coefficients",
    )(*args)


def far_pack_kernel(
    arrived_ref, columns_ref, out_hbm, out_ref, ask_ref, cluster_ref, sem, out_sem
):
    (copy,) = fetch(sem, (arrived_ref.at[:, pl.ds(ASK, NEAR_MESSAGE - ASK)], ask_ref))
    left = lax.broadcasted_iota(jnp.int32, (ROWS, 2 * RANK), 1) < RANK
    for pair in range(PAIRS):
        wide = columns_ref[pair].astype(jnp.float32)
        turned = pltpu.roll(wide, RANK, 1)
        cluster_ref[2 * pair] = jnp.where(left, wide, turned)
        cluster_ref[2 * pair + 1] = jnp.where(left, turned, wide)
    wide = columns_ref[PAIRS].astype(jnp.float32)
    turned = pltpu.roll(wide, RANK, 1)
    half = left[:HALF_ROWS]
    second = (
        jnp.where(half, wide[:HALF_ROWS], turned[HALF_ROWS:]),
        jnp.where(half, turned[:HALF_ROWS], wide[HALF_ROWS:]),
    )
    copy.wait()

    def fill(chip, _):
        for core in range(2):
            peer = 2 * chip + core
            wanted = ask_ref[peer].astype(jnp.float32)[:8]
            wanted = jnp.concatenate([wanted] * (ROWS // 8), axis=0)
            first = cluster_ref[0]
            for c in range(1, ONE):
                first = jnp.where(wanted == c, cluster_ref[c], first)
            out_ref[peer] = jnp.concatenate([first, second[core]], axis=0).astype(jnp.bfloat16)
        return 0

    sent = []
    for part in range(4):
        lax.fori_loop(part * PEERS // 8, (part + 1) * PEERS // 8, fill, 0, unroll=4)
        peers = pl.ds(part * PEERS // 4, PEERS // 4)
        sent.append(pltpu.make_async_copy(out_ref.at[peers], out_hbm.at[peers], out_sem.at[part]))
        sent[-1].start()
    for copy in sent:
        copy.wait()


def far_pack(arrived, columns):
    return pl.pallas_call(
        far_pack_kernel,
        out_shape=jax.ShapeDtypeStruct((PEERS, MESSAGE, 2 * RANK), jnp.bfloat16),
        in_specs=[ANY, VM],
        out_specs=ANY,
        scratch_shapes=[
            bf16(PEERS, MESSAGE, 2 * RANK),
            bf16(PEERS, NEAR_MESSAGE - ASK, 2 * RANK),
            pltpu.VMEM((ONE, ROWS, 2 * RANK), jnp.float32),
            pltpu.SemaphoreType.DMA((1,)),
            pltpu.SemaphoreType.DMA((4,)),
        ],
        compiler_params=vmem(56),
        cost_estimate=cost(1 << 20, 5 * MIB),
        name="far_pack",
    )(arrived, columns)


def table_rows(near_source, me):
    mine = lax.dynamic_slice_in_dim(near_source, me * LEAVES, LEAVES, 0).reshape(-1)
    device, leaf = mine >> 5, mine & 31
    from_peer = device[:, None] == jnp.arange(PEERS, dtype=jnp.int32)[None, :]
    low = jnp.min(jnp.where(from_peer, leaf[:, None], LEAVES), axis=0)
    high = jnp.max(jnp.where(from_peer, leaf[:, None], -1), axis=0)
    low_of = jnp.sum(jnp.where(from_peer, low[None, :], 0), axis=1)
    high_of = jnp.sum(jnp.where(from_peer, high[None, :], 0), axis=1)
    row = device + PEERS * (leaf != low_of)
    inner = (leaf > low_of) & (leaf < high_of)
    for side, step in enumerate((PEERS - 1, 1)):
        chosen = inner & (device == (me + step) % PEERS)
        first = jnp.min(jnp.where(chosen, leaf, LEAVES))
        row = jnp.where(chosen, 2 * PEERS + 2 * side + (leaf != first), row)
    return jnp.where(device == me, LOCAL + leaf, row)


def with_square(block, first):
    wide = block.astype(jnp.float32)
    square = jnp.sum(wide * wide, axis=0, keepdims=True) * -2
    high = square.astype(jnp.bfloat16).astype(jnp.float32)
    middle = (square - high).astype(jnp.bfloat16).astype(jnp.float32)
    low = square - high - middle
    at = lax.broadcasted_iota(jnp.int32, (16, LEAF), 0)
    ones, parts = (3, 0) if first else (0, 3)
    extra = jnp.where((at >= ones) & (at < ones + 3), 1.0, 0.0)
    for i, part in enumerate((high, middle, low)):
        extra = jnp.where(at == parts + i, part, extra)
    if first:
        return jnp.concatenate([wide * 4, extra], axis=0).T.astype(jnp.bfloat16)
    return jnp.concatenate([block, extra.astype(jnp.bfloat16)], axis=0)


def points_of(block):
    return jnp.concatenate([block[:DIM], block[ROWS : ROWS + DIM]], axis=1)


def rhs_of(block):
    return jnp.concatenate([block[DIM:ROWS], block[ROWS + DIM :]], axis=1)


def turn_targets(own_ref, target_ref):
    def turn(leaf, _):
        target_ref[leaf, :, :ROWS] = with_square(points_of(own_ref[leaf]), True)
        return 0

    lax.fori_loop(0, LEAVES, turn, 0, unroll=2)


def add_pairs(list_ref, start, table_ref, target_ref, out_ref):
    def step(i, _):
        pairs = []
        for u in range(GROUP):
            pair = list_ref[start + i * GROUP + u]
            target, row = pair // STRIDE, pair & (STRIDE - 1)
            weights = jnp.exp(
                dot(target_ref[target, :, :ROWS], with_square(points_of(table_ref[row]), False))
            ).astype(jnp.bfloat16)
            pairs.append((target, row, weights))
        terms = [(t, dot(rhs_of(table_ref[row]), weights, NT)) for t, row, weights in pairs]
        for target, term in terms:
            columns = pl.ds(pl.multiple_of(target * LEAF, LEAF), LEAF)
            out_ref[:, columns] += term
        return 0

    lax.fori_loop(0, (list_ref[start + LIST - 1] + GROUP - 1) // GROUP, step, 0)


def own_kernel(row_ref, own_hbm, out_ref, list_ref, own_ref, target_ref, sem):
    (copy,) = fetch(sem, (own_hbm, own_ref.at[pl.ds(0, LEAVES)]))

    def sort(target, counts):
        mine, others = counts
        for k in range(NEAR):
            row = row_ref[target * NEAR + k]
            list_ref[mine] = target * STRIDE + jnp.maximum(row - LOCAL, 0)
            list_ref[LIST + others] = target * STRIDE + row
            is_mine = (row >= LOCAL).astype(jnp.int32)
            mine, others = mine + is_mine, others + 1 - is_mine
        return mine, others

    mine, others = lax.fori_loop(0, LEAVES, sort, (jnp.int32(0), jnp.int32(0)))
    for u in range(GROUP):
        list_ref[mine + u] = LEAVES
        list_ref[LIST + others + u] = LOCAL
    list_ref[LIST - 1] = mine
    list_ref[2 * LIST - 1] = others
    own_ref[LEAVES] = jnp.zeros((BLOCK, 128), jnp.bfloat16)
    copy.wait()
    turn_targets(own_ref, target_ref)
    out_ref[...] = jnp.zeros_like(out_ref)
    add_pairs(list_ref, 0, own_ref, target_ref, out_ref)


def own_pairs(rows, own):
    return pl.pallas_call(
        own_kernel,
        out_shape=(
            jax.ShapeDtypeStruct((NRHS, LEAVES * LEAF), jnp.float32),
            jax.ShapeDtypeStruct((2 * LIST,), jnp.int32),
        ),
        in_specs=[SM, ANY],
        out_specs=(VM, SM),
        scratch_shapes=[
            bf16(LEAVES + 1, BLOCK, 128),
            bf16(LEAVES, LEAF, 128),
            pltpu.SemaphoreType.DMA((1,)),
        ],
        compiler_params=vmem(24),
        cost_estimate=cost(2 * 120 * 65536 * 272, 2 * MIB, 120 * 65536),
        name="own_pairs",
    )(rows, own)


def remote_kernel(
    list_ref, arrived_ref, left_ref, right_ref, own_hbm, field_ref, out_ref,
    table_ref, own_ref, target_ref, sem,
):
    near = fetch(
        sem,
        (own_hbm, own_ref),
        (field_ref, out_ref),
        (arrived_ref.at[:, pl.ds(0, BLOCK)], table_ref.at[pl.ds(0, PEERS)]),
        (arrived_ref.at[:, pl.ds(BLOCK, BLOCK)], table_ref.at[pl.ds(PEERS, PEERS)]),
        (left_ref, table_ref.at[pl.ds(2 * PEERS, 2)]),
        (right_ref, table_ref.at[pl.ds(2 * PEERS + 2, 2)]),
    )
    table_ref[LOCAL] = jnp.zeros((BLOCK, 128), jnp.bfloat16)
    near[0].wait()
    turn_targets(own_ref, target_ref)
    for copy in near[1:]:
        copy.wait()
    add_pairs(list_ref, LIST, table_ref, target_ref, out_ref)


def remote_pairs(lists, arrived, left, right, own, field):
    return pl.pallas_call(
        remote_kernel,
        out_shape=jax.ShapeDtypeStruct((NRHS, LEAVES * LEAF), jnp.float32),
        in_specs=[SM, ANY, ANY, ANY, ANY, ANY],
        out_specs=VM,
        scratch_shapes=[
            bf16(LOCAL + 1, BLOCK, 128),
            bf16(LEAVES, BLOCK, 128),
            bf16(LEAVES, LEAF, 128),
            pltpu.SemaphoreType.DMA((6,)),
        ],
        compiler_params=vmem(32),
        cost_estimate=cost(2 * 200 * 65536 * 272, 8 * MIB, 200 * 65536),
        name="remote_pairs",
    )(lists, arrived, left, right, own, field)


def turned(skel_ref, pair):
    return skel_ref[:, pl.ds(pair * 2 * RANK, 2 * RANK)].astype(jnp.float32).T


def field_pair(targets, blocks, halves):
    half_of = lax.broadcasted_iota(jnp.int32, (NRHS, 2 * RANK), 1) >> 6
    total = None
    for i, padded in enumerate((upper, below)):
        target = targets[i * RANK : (i + 1) * RANK]
        target_sq = jnp.sum(target * target, axis=1, keepdims=True) * 2
        source = jnp.concatenate([block[:DIM] for block in blocks[i]], axis=1)
        coeffs = jnp.concatenate(
            [
                jnp.where(half_of == half, block[DIM:], 0)
                for block, half in zip(blocks[i], halves[i], strict=True)
            ],
            axis=1,
        )
        wide = source.astype(jnp.float32)
        source_sq = jnp.sum(wide * wide, axis=0, keepdims=True) * 2
        power = dot((target * 4).astype(jnp.bfloat16), source) - target_sq - source_sq
        weights = jnp.exp(power).astype(jnp.bfloat16)
        term = dot(coeffs, padded(weights), NT)
        total = term if i == 0 else total + term
    return total


def far_one_kernel(
    far_ref, low_ref, arrived_ref, skel_hbm, near_hbm, one_hbm, out_ref, near_ref, one_ref, skel_ref,
    in_sem,
):
    copy, *brought = fetch(in_sem, (skel_hbm, skel_ref), (near_hbm, near_ref), (one_hbm, one_ref))
    copy.wait()
    for pair in range(PAIRS):
        clusters = (2 * pair, 2 * pair + 1)
        blocks = [
            [arrived_ref[far_ref[c, j] >> 3, :ROWS, :] for j in range(FAR)] for c in clusters
        ]
        halves = [
            [
                ((far_ref[c, j] & 7) != low_ref[0, far_ref[c, j] >> 3]).astype(jnp.int32)
                for j in range(FAR)
            ]
            for c in clusters
        ]
        out_ref[pair] = field_pair(turned(skel_ref, pair), blocks, halves)
    for copy in brought:
        copy.wait()


def far_one_field(far_one, low, arrived, skeleton_one, near, transfer_one):
    return pl.pallas_call(
        far_one_kernel,
        out_shape=(
            jax.ShapeDtypeStruct((PAIRS, NRHS, 2 * RANK), jnp.float32),
            jax.ShapeDtypeStruct(near.shape, near.dtype),
            jax.ShapeDtypeStruct(transfer_one.shape, transfer_one.dtype),
        ),
        in_specs=[SM, SM, VM, ANY, ANY, ANY],
        out_specs=(VM, VM, VM),
        scratch_shapes=[bf16(DIM, ONE * RANK), pltpu.SemaphoreType.DMA((3,))],
        compiler_params=vmem(16),
        cost_estimate=cost(1 << 28, 2 * MIB, 1 << 19),
        name="far_one_field",
    )(far_one, low, arrived, skeleton_one, near, transfer_one)


def final_kernel(
    far_ref, mine_ref, theirs_ref, field_one_ref, near_ref, one_ref, skel_hbm, two_hbm, basis_hbm,
    out_ref, skel_ref, two_ref, basis_ref, in_sem,
):
    core = lax.rem(lax.axis_index("leaf"), 2)
    skel_copy, two_copy, basis_copy = fetch(
        in_sem, (skel_hbm, skel_ref), (two_hbm, two_ref), (basis_hbm, basis_ref)
    )

    def split(x):
        high = x.astype(jnp.bfloat16)
        return jnp.concatenate([high, (x - high.astype(jnp.float32)).astype(jnp.bfloat16)], axis=0)

    def exact(parts, b):
        both = dot(parts, b)
        return both[:NRHS] + both[NRHS:]

    def whole(e, j):
        b = far_ref[e, j]
        rows = jnp.where((b & 1) == core, mine_ref[b >> 1], theirs_ref[b >> 1]).astype(jnp.float32)
        return jnp.concatenate([rows, pltpu.roll(rows, RANK, 1)], axis=0).astype(jnp.bfloat16)

    blocks = [[whole(e, j) for j in range(FAR)] for e in range(TWO)]
    skel_copy.wait()
    field_two = split(field_pair(turned(skel_ref, 0), blocks, [[0] * FAR] * TWO))
    two_copy.wait()
    from_two = [
        exact(field_two, padded(two_ref[e])) for e, padded in enumerate((upper, below))
    ]
    down_leaf = []
    for pair in range(PAIRS):
        parent = from_two[pair // 2][:, (pair % 2) * 2 * RANK : (pair % 2 + 1) * 2 * RANK]
        down_one = split(field_one_ref[pair] + parent)
        for i, padded in enumerate((upper, below)):
            down_leaf.append(exact(down_one, padded(one_ref[2 * pair + i])).astype(jnp.bfloat16))
    basis_copy.wait()
    for leaf in range(LEAVES):
        columns = pl.ds(leaf * LEAF, LEAF)
        at = (leaf % 4) // 2
        half = down_leaf[leaf // 4][:, at * 2 * RANK : (at + 1) * 2 * RANK]
        basis = (upper, below)[leaf % 2](basis_ref[:, columns])
        out_ref[:, columns] = (near_ref[:, columns] + dot(half, basis)).astype(jnp.bfloat16)


def finish(far_two, mine, theirs, field_one, near, transfer_one, *arrays):
    return pl.pallas_call(
        final_kernel,
        out_shape=jax.ShapeDtypeStruct((NRHS, LEAVES * LEAF), jnp.bfloat16),
        in_specs=[SM] + [VM] * 5 + [ANY] * 3,
        out_specs=VM,
        scratch_shapes=[bf16(*a.shape) for a in arrays] + [pltpu.SemaphoreType.DMA((3,))],
        compiler_params=vmem(16),
        cost_estimate=cost(1 << 28, 3 * MIB, 1 << 17),
        name="finish",
    )(far_two, mine, theirs, field_one, near, transfer_one, *arrays)


def shift(x, step):
    return lax.ppermute(x, "leaf", [(i, (i + step) % PEERS) for i in range(PEERS)])


def swap(x):
    return lax.ppermute(x, "leaf", [(i, i ^ 1) for i in range(PEERS)])


def exchange(x):
    return lax.all_to_all(x, "leaf", split_axis=0, concat_axis=0, tiled=True)


def local(
    points, rhs, basis, transfer_one, transfer_two, skeleton_one, skeleton_two, near_source,
    far_one, far_two,
):
    me = lax.axis_index("leaf")
    message, to_right, to_left, own, low = pack(near_source, far_one, points, rhs)
    arrived = exchange(message)
    columns = coefficients(rhs, basis, transfer_one, transfer_two, skeleton_one, skeleton_two)
    field, lists = own_pairs(table_rows(near_source, me), own)
    to_right, to_left, columns, field, lists = lax.optimization_barrier(
        (to_right, to_left, columns, field, lists)
    )
    from_left, from_right = shift(to_right, 1), shift(to_left, -1)
    arrived, from_left, from_right = lax.optimization_barrier((arrived, from_left, from_right))
    far_arrived = exchange(far_pack(arrived, columns))
    near = remote_pairs(lists, arrived, from_left, from_right, own, field)
    far_arrived, near = lax.optimization_barrier((far_arrived, near))
    mine = far_arrived[:, ROWS:, :]
    theirs = swap(mine)
    near = pltpu.with_memory_space_constraint(near, pltpu.HBM)
    transfer_one = pltpu.with_memory_space_constraint(transfer_one, pltpu.HBM)
    field_one, near, transfer_one = far_one_field(
        far_one, low, far_arrived, skeleton_one, near, transfer_one
    )
    return finish(
        far_two, mine, theirs, field_one, near, transfer_one, skeleton_two, transfer_two, basis
    )


def solution(mesh):
    placed = (
        P(None, "leaf"),
        P(None, "leaf"),
        P(None, "leaf"),
        P("leaf", None, None),
        P("leaf", None, None),
        P(None, "leaf"),
        P(None, "leaf"),
        P(),
        P("leaf", None),
        P("leaf", None),
    )
    return jax.shard_map(
        local, mesh=mesh, in_specs=placed, out_specs=P(None, "leaf"), check_vma=False
    )
```

```python
import jax
import jax.numpy as jnp
from jax import lax
from jax.experimental import pallas as pl
from jax.experimental.pallas import tpu as pltpu
from jax.sharding import PartitionSpec as P

DIM = 32
NRHS = 16
RANK = 64
LEAF = 256
NEAR = 10
FAR = 8
LEAVES = 32
ONE = 8
TWO = 2
PAIRS = ONE // 2
ROWS = DIM + NRHS
PEERS = 128
LOCAL = 2 * PEERS + 4
TABLE = LOCAL + LEAVES
GROUP = 16
LIST = 384
STRIDE = 512
HALF_ROWS = ROWS // 2
MESSAGE = ROWS + HALF_ROWS - 8
BLOCK = 2 * ROWS
ASK = 2 * BLOCK
NEAR_MESSAGE = ASK + 16
MIB = 1 << 20

NT = (((1,), (1,)), ((), ()))
NN = (((1,), (0,)), ((), ()))


def dot(a, b, dims=NN):
    return lax.dot_general(a, b, dims, preferred_element_type=jnp.float32)


def vmem(limit):
    return pltpu.CompilerParams(vmem_limit_bytes=limit * MIB)


def cost(flops, moved, exps=0):
    return pl.CostEstimate(flops=flops, bytes_accessed=moved, transcendentals=exps)


def fetch(sem, *pairs):
    copies = [pltpu.make_async_copy(a, b, sem.at[i]) for i, (a, b) in enumerate(pairs)]
    for copy in copies:
        copy.start()
    return copies


def bf16(*shape):
    return pltpu.VMEM(shape, jnp.bfloat16)


ANY = pl.BlockSpec(memory_space=pl.ANY)
VM = pl.BlockSpec(memory_space=pltpu.VMEM)
SM = pl.BlockSpec(memory_space=pltpu.SMEM)


def pack_kernel(
    source_ref, far_ref, skel_ref, points_ref, rhs_ref, msg_ref, right_ref, left_ref, own_ref, low_ref,
    lists_ref, points_vmem, rhs_vmem, block_ref, ask_ref, row_ref, row_smem,
    in_sem, row_sem, ask_sem, msg_sem, side_sem,
):
    me = lax.axis_index("leaf")
    listed = pltpu.make_async_copy(source_ref, lists_ref, row_sem)
    listed.start()
    filled = fetch(in_sem, (points_ref, points_vmem), (rhs_ref, rhs_vmem))
    peer = lax.broadcasted_iota(jnp.int32, (PEERS, FAR), 0) * ONE
    low = high = None
    for i in range(ONE):
        at = far_ref[i : i + 1, :] - peer
        inside = (at >> 3) == 0
        a, b = jnp.where(inside, at, ONE), jnp.where(inside, at, -1)
        low = a if i == 0 else jnp.minimum(low, a)
        high = b if i == 0 else jnp.maximum(high, b)
    low = jnp.min(low.astype(jnp.float32), axis=1, keepdims=True)
    high = jnp.max(high.astype(jnp.float32), axis=1, keepdims=True)
    lane = lax.broadcasted_iota(jnp.int32, (PEERS, PEERS), 1)
    wanted = jnp.where(lane < RANK, low, high)
    wide = skel_ref[...].astype(jnp.float32)
    turned = pltpu.roll(wide, RANK, 1)
    left = lane[:8] < RANK
    tops = (
        jnp.where(left, wide[:8], turned[HALF_ROWS:]),
        jnp.where(left, turned[:8], wide[HALF_ROWS:]),
    )
    core = lax.broadcasted_iota(jnp.int32, (PEERS, 8, 2 * RANK), 0) & 1
    ask_ref[...] = jnp.concatenate(
        [
            jnp.broadcast_to(wanted[:, None, :], core.shape),
            jnp.where(core == 0, tops[0][None], tops[1][None]),
        ],
        axis=1,
    ).astype(jnp.bfloat16)
    asked = pltpu.make_async_copy(ask_ref, msg_ref.at[:, pl.ds(ASK, NEAR_MESSAGE - ASK)], ask_sem)
    asked.start()
    across = lax.broadcasted_iota(jnp.int32, (ONE, PEERS), 1) * ONE
    low = None
    for j in range(FAR):
        at = far_ref[:, j : j + 1] - across
        a = jnp.where((at >> 3) == 0, at, ONE)
        low = a if j == 0 else jnp.minimum(low, a)
    low = jnp.min(low.astype(jnp.float32), axis=0, keepdims=True)
    low_ref[...] = jnp.broadcast_to(low, (ONE, PEERS)).astype(jnp.int32)
    listed.wait()
    width = PEERS * LEAVES
    def marks(lists):
        mine = lists - me * LEAVES
        inside = (mine >> 5) == 0
        return (
            jnp.where(inside, mine, LEAVES),
            jnp.where(inside, -mine, 1),
            jnp.where(inside, 1 << (mine & 31), 0),
        )

    low, high, bits = marks(lists_ref[:8, :])
    for k in range(8, NEAR):
        a, b, c = (jnp.broadcast_to(v, (8, width)) for v in marks(lists_ref[k : k + 1, :]))
        low, high, bits = jnp.minimum(low, a), jnp.minimum(high, b), bits | c
    for step in (4, 2, 1):
        low = jnp.minimum(low, pltpu.roll(low, step, 0))
        high = jnp.minimum(high, pltpu.roll(high, step, 0))
        bits = bits | pltpu.roll(bits, step, 0)
    upper_rows = lax.broadcasted_iota(jnp.int32, (8, width), 0) < 4
    both = jnp.where(upper_rows, low, high)
    for step in (16, 8, 4, 2, 1):
        both = jnp.minimum(both, pltpu.roll(both, width - step, 1))
        bits = bits | pltpu.roll(bits, width - step, 1)
    low, high = both, -pltpu.roll(both, 4, 0)
    place = lax.broadcasted_iota(jnp.int32, (8, width), 1) & 31
    row_ref[...] = jnp.where(
        place == 0, low, jnp.where(place == 1, pltpu.roll(high, 1, 1), pltpu.roll(bits, 2, 1))
    )
    copy = pltpu.make_async_copy(row_ref.at[0:1], row_smem, row_sem)
    copy.start()
    for fill in filled:
        fill.wait()
    for leaf in range(LEAVES):
        for half in range(2):
            columns = pl.ds(leaf * LEAF + half * 128, 128)
            block_ref[leaf, pl.ds(half * ROWS, DIM), :] = points_vmem[:, columns]
            block_ref[leaf, pl.ds(half * ROWS + DIM, NRHS), :] = rhs_vmem[:, columns]
    own = pltpu.make_async_copy(block_ref, own_ref, in_sem.at[0])
    own.start()
    copy.wait()

    def send(peer, _):
        for slot in range(2):
            leaf = row_smem[0, peer * LEAVES + slot] & 31
            pltpu.make_async_copy(
                block_ref.at[leaf], msg_ref.at[peer, pl.ds(slot * BLOCK, BLOCK)], msg_sem
            ).start()
        return 0

    lax.fori_loop(0, PEERS, send, 0, unroll=8)
    for side, (ref, step) in enumerate(((right_ref, 1), (left_ref, PEERS - 1))):
        at = lax.rem(me + step, PEERS) * LEAVES
        between = row_smem[0, at + 2]
        between = between & ~(1 << (row_smem[0, at] & 31)) & ~(1 << (row_smem[0, at + 1] & 31))

        def scan(bit, found):
            has = ((between >> bit) & 1) == 1
            return jnp.where(has & (found[0] < 0), bit, found[0]), jnp.where(has, bit, found[1])

        first, last = lax.fori_loop(0, LEAVES, scan, (jnp.int32(-1), jnp.int32(0)))
        for slot, leaf in enumerate((first & 31, last & 31)):
            pltpu.make_async_copy(block_ref.at[leaf], ref.at[slot], side_sem.at[side]).start()
    sent = msg_ref.at[:, pl.ds(0, ASK)]
    pltpu.make_async_copy(sent, sent, msg_sem).wait()
    asked.wait()
    for side, ref in enumerate((right_ref, left_ref)):
        pltpu.make_async_copy(ref, ref, side_sem.at[side]).wait()
    own.wait()


def pack(source, far_one, skeleton_two, points, rhs):
    block = jax.ShapeDtypeStruct((LEAVES, BLOCK, 128), jnp.bfloat16)
    side = jax.ShapeDtypeStruct((2, BLOCK, 128), jnp.bfloat16)
    return pl.pallas_call(
        pack_kernel,
        out_shape=(
            jax.ShapeDtypeStruct((PEERS, NEAR_MESSAGE, 128), jnp.bfloat16), side, side, block,
            jax.ShapeDtypeStruct((ONE, PEERS), jnp.int32),
        ),
        in_specs=[ANY, VM, VM, ANY, ANY],
        out_specs=(ANY, ANY, ANY, ANY, VM),
        scratch_shapes=[
            pltpu.VMEM((NEAR, PEERS * LEAVES), jnp.int32),
            bf16(*points.shape),
            bf16(*rhs.shape),
            bf16(LEAVES, BLOCK, 128),
            bf16(PEERS, NEAR_MESSAGE - ASK, 2 * RANK),
            pltpu.VMEM((8, PEERS * LEAVES), jnp.int32),
            pltpu.SMEM((1, PEERS * LEAVES), jnp.int32),
            pltpu.SemaphoreType.DMA((2,)),
            pltpu.SemaphoreType.DMA,
            pltpu.SemaphoreType.DMA,
            pltpu.SemaphoreType.DMA,
            pltpu.SemaphoreType.DMA((2,)),
        ],
        compiler_params=vmem(56),
        cost_estimate=cost(1 << 20, 14 * MIB),
        name="pack",
    )(source.T, far_one, skeleton_two, points, rhs)


def upper(b):
    return jnp.concatenate([b, jnp.zeros_like(b)], axis=0)


def below(b):
    return jnp.concatenate([jnp.zeros_like(b), b], axis=0)


def coeff_kernel(
    rhs_hbm, basis_hbm, one_hbm, two_hbm, skel_one_hbm, skel_two_hbm, out_ref,
    rhs_ref, basis_ref, one_ref, two_ref, skel_one_ref, skel_two_ref, sem,
):
    for copy in fetch(
        sem, (rhs_hbm, rhs_ref), (basis_hbm, basis_ref), (one_hbm, one_ref), (two_hbm, two_ref),
        (skel_one_hbm, skel_one_ref), (skel_two_hbm, skel_two_ref),
    ):
        copy.wait()

    def leaf_pair(leaf):
        a, b = (pl.ds((leaf + i) * LEAF, LEAF) for i in range(2))
        return (
            dot(rhs_ref[:, a], upper(basis_ref[:, a]), NT)
            + dot(rhs_ref[:, b], below(basis_ref[:, b]), NT)
        ).astype(jnp.bfloat16)

    def lift_pair(children, transfer_ref, cluster):
        return (
            dot(children[0], upper(transfer_ref[cluster]), NT)
            + dot(children[1], below(transfer_ref[cluster + 1]), NT)
        ).astype(jnp.bfloat16)

    pairs = []
    for pair in range(PAIRS):
        joined = [
            jnp.concatenate([leaf_pair(4 * c), leaf_pair(4 * c + 2)], axis=1)
            for c in (2 * pair, 2 * pair + 1)
        ]
        pairs.append(lift_pair(joined, one_ref, 2 * pair))
        out_ref[pair, :DIM, :] = skel_one_ref[:, pl.ds(pair * 2 * RANK, 2 * RANK)]
        out_ref[pair, DIM:, :] = pairs[-1]
    joined = [jnp.concatenate(pairs[2 * e : 2 * e + 2], axis=1) for e in range(TWO)]
    out_ref[PAIRS, :DIM, :] = skel_two_ref[...]
    out_ref[PAIRS, DIM:, :] = lift_pair(joined, two_ref, 0)


def coefficients(*args):
    return pl.pallas_call(
        coeff_kernel,
        out_shape=jax.ShapeDtypeStruct((PAIRS + 1, ROWS, 2 * RANK), jnp.bfloat16),
        in_specs=[ANY] * 6,
        out_specs=VM,
        scratch_shapes=[bf16(*a.shape) for a in args] + [pltpu.SemaphoreType.DMA((6,))],
        compiler_params=vmem(24),
        cost_estimate=cost(1 << 26, 2 * MIB),
        name="coefficients",
    )(*args)


def far_pack_kernel(
    arrived_ref, columns_ref, out_hbm, out_ref, ask_ref, cluster_ref, sem, out_sem
):
    (copy,) = fetch(sem, (arrived_ref.at[:, pl.ds(ASK, NEAR_MESSAGE - ASK)], ask_ref))
    left = lax.broadcasted_iota(jnp.int32, (ROWS, 2 * RANK), 1) < RANK
    for pair in range(PAIRS):
        wide = columns_ref[pair].astype(jnp.float32)
        turned = pltpu.roll(wide, RANK, 1)
        cluster_ref[2 * pair] = jnp.where(left, wide, turned)
        cluster_ref[2 * pair + 1] = jnp.where(left, turned, wide)
    wide = columns_ref[PAIRS].astype(jnp.float32)
    turned = pltpu.roll(wide, RANK, 1)
    half = left[:HALF_ROWS]
    second = (
        jnp.where(half, wide[:HALF_ROWS], turned[HALF_ROWS:]),
        jnp.where(half, turned[:HALF_ROWS], wide[HALF_ROWS:]),
    )
    copy.wait()

    def fill(chip, _):
        for core in range(2):
            peer = 2 * chip + core
            wanted = ask_ref[peer].astype(jnp.float32)[:8]
            wanted = jnp.concatenate([wanted] * (ROWS // 8), axis=0)
            first = cluster_ref[0]
            for c in range(1, ONE):
                first = jnp.where(wanted == c, cluster_ref[c], first)
            out_ref[peer] = jnp.concatenate([first, second[core][8:]], axis=0).astype(jnp.bfloat16)
        return 0

    sent = []
    for part in range(4):
        lax.fori_loop(part * PEERS // 8, (part + 1) * PEERS // 8, fill, 0, unroll=4)
        peers = pl.ds(part * PEERS // 4, PEERS // 4)
        sent.append(pltpu.make_async_copy(out_ref.at[peers], out_hbm.at[peers], out_sem.at[part]))
        sent[-1].start()
    for copy in sent:
        copy.wait()


def far_pack(arrived, columns):
    return pl.pallas_call(
        far_pack_kernel,
        out_shape=jax.ShapeDtypeStruct((PEERS, MESSAGE, 2 * RANK), jnp.bfloat16),
        in_specs=[ANY, VM],
        out_specs=ANY,
        scratch_shapes=[
            bf16(PEERS, MESSAGE, 2 * RANK),
            bf16(PEERS, NEAR_MESSAGE - ASK, 2 * RANK),
            pltpu.VMEM((ONE, ROWS, 2 * RANK), jnp.float32),
            pltpu.SemaphoreType.DMA((1,)),
            pltpu.SemaphoreType.DMA((4,)),
        ],
        compiler_params=vmem(56),
        cost_estimate=cost(1 << 20, 5 * MIB),
        name="far_pack",
    )(arrived, columns)


def table_rows(near_source, me):
    mine = lax.dynamic_slice_in_dim(near_source, me * LEAVES, LEAVES, 0).reshape(-1)
    device, leaf = mine >> 5, mine & 31
    from_peer = device[:, None] == jnp.arange(PEERS, dtype=jnp.int32)[None, :]
    low = jnp.min(jnp.where(from_peer, leaf[:, None], LEAVES), axis=0)
    high = jnp.max(jnp.where(from_peer, leaf[:, None], -1), axis=0)
    low_of = jnp.sum(jnp.where(from_peer, low[None, :], 0), axis=1)
    high_of = jnp.sum(jnp.where(from_peer, high[None, :], 0), axis=1)
    row = device + PEERS * (leaf != low_of)
    inner = (leaf > low_of) & (leaf < high_of)
    for side, step in enumerate((PEERS - 1, 1)):
        chosen = inner & (device == (me + step) % PEERS)
        first = jnp.min(jnp.where(chosen, leaf, LEAVES))
        row = jnp.where(chosen, 2 * PEERS + 2 * side + (leaf != first), row)
    return jnp.where(device == me, LOCAL + leaf, row)


def with_square(block, first):
    wide = block.astype(jnp.float32)
    square = jnp.sum(wide * wide, axis=0, keepdims=True) * -2
    high = square.astype(jnp.bfloat16).astype(jnp.float32)
    middle = (square - high).astype(jnp.bfloat16).astype(jnp.float32)
    low = square - high - middle
    at = lax.broadcasted_iota(jnp.int32, (16, LEAF), 0)
    ones, parts = (3, 0) if first else (0, 3)
    extra = jnp.where((at >= ones) & (at < ones + 3), 1.0, 0.0)
    for i, part in enumerate((high, middle, low)):
        extra = jnp.where(at == parts + i, part, extra)
    if first:
        return jnp.concatenate([wide * 4, extra], axis=0).T.astype(jnp.bfloat16)
    return jnp.concatenate([block, extra.astype(jnp.bfloat16)], axis=0)


def points_of(block):
    return jnp.concatenate([block[:DIM], block[ROWS : ROWS + DIM]], axis=1)


def rhs_of(block):
    return jnp.concatenate([block[DIM:ROWS], block[ROWS + DIM :]], axis=1)


def turn_targets(own_ref, target_ref):
    def turn(leaf, _):
        target_ref[leaf, :, :ROWS] = with_square(points_of(own_ref[leaf]), True)
        return 0

    lax.fori_loop(0, LEAVES, turn, 0, unroll=2)


def add_pairs(list_ref, start, table_ref, target_ref, out_ref):
    def step(i, _):
        pairs = []
        for u in range(GROUP):
            pair = list_ref[start + i * GROUP + u]
            target, row = pair // STRIDE, pair & (STRIDE - 1)
            weights = jnp.exp(
                dot(target_ref[target, :, :ROWS], with_square(points_of(table_ref[row]), False))
            ).astype(jnp.bfloat16)
            pairs.append((target, row, weights))
        terms = [(t, dot(rhs_of(table_ref[row]), weights, NT)) for t, row, weights in pairs]
        for target, term in terms:
            columns = pl.ds(pl.multiple_of(target * LEAF, LEAF), LEAF)
            out_ref[:, columns] += term
        return 0

    lax.fori_loop(0, (list_ref[start + LIST - 1] + GROUP - 1) // GROUP, step, 0)


def own_kernel(row_ref, own_hbm, out_ref, list_ref, own_ref, target_ref, sem):
    (copy,) = fetch(sem, (own_hbm, own_ref.at[pl.ds(0, LEAVES)]))

    def sort(target, counts):
        mine, others = counts
        for k in range(NEAR):
            row = row_ref[target * NEAR + k]
            list_ref[mine] = target * STRIDE + jnp.maximum(row - LOCAL, 0)
            list_ref[LIST + others] = target * STRIDE + row
            is_mine = (row >= LOCAL).astype(jnp.int32)
            mine, others = mine + is_mine, others + 1 - is_mine
        return mine, others

    mine, others = lax.fori_loop(0, LEAVES, sort, (jnp.int32(0), jnp.int32(0)))
    for u in range(GROUP):
        list_ref[mine + u] = LEAVES
        list_ref[LIST + others + u] = LOCAL
    list_ref[LIST - 1] = mine
    list_ref[2 * LIST - 1] = others
    own_ref[LEAVES] = jnp.zeros((BLOCK, 128), jnp.bfloat16)
    copy.wait()
    turn_targets(own_ref, target_ref)
    out_ref[...] = jnp.zeros_like(out_ref)
    add_pairs(list_ref, 0, own_ref, target_ref, out_ref)


def own_pairs(rows, own):
    return pl.pallas_call(
        own_kernel,
        out_shape=(
            jax.ShapeDtypeStruct((NRHS, LEAVES * LEAF), jnp.float32),
            jax.ShapeDtypeStruct((2 * LIST,), jnp.int32),
        ),
        in_specs=[SM, ANY],
        out_specs=(VM, SM),
        scratch_shapes=[
            bf16(LEAVES + 1, BLOCK, 128),
            bf16(LEAVES, LEAF, 128),
            pltpu.SemaphoreType.DMA((1,)),
        ],
        compiler_params=vmem(24),
        cost_estimate=cost(2 * 120 * 65536 * 272, 2 * MIB, 120 * 65536),
        name="own_pairs",
    )(rows, own)


def remote_kernel(
    list_ref, arrived_ref, left_ref, right_ref, own_hbm, field_ref, out_ref,
    table_ref, own_ref, target_ref, sem,
):
    near = fetch(
        sem,
        (own_hbm, own_ref),
        (field_ref, out_ref),
        (arrived_ref.at[:, pl.ds(0, BLOCK)], table_ref.at[pl.ds(0, PEERS)]),
        (arrived_ref.at[:, pl.ds(BLOCK, BLOCK)], table_ref.at[pl.ds(PEERS, PEERS)]),
        (left_ref, table_ref.at[pl.ds(2 * PEERS, 2)]),
        (right_ref, table_ref.at[pl.ds(2 * PEERS + 2, 2)]),
    )
    table_ref[LOCAL] = jnp.zeros((BLOCK, 128), jnp.bfloat16)
    near[0].wait()
    turn_targets(own_ref, target_ref)
    for copy in near[1:]:
        copy.wait()
    add_pairs(list_ref, LIST, table_ref, target_ref, out_ref)


def remote_pairs(lists, arrived, left, right, own, field):
    return pl.pallas_call(
        remote_kernel,
        out_shape=jax.ShapeDtypeStruct((NRHS, LEAVES * LEAF), jnp.float32),
        in_specs=[SM, ANY, ANY, ANY, ANY, ANY],
        out_specs=VM,
        scratch_shapes=[
            bf16(LOCAL + 1, BLOCK, 128),
            bf16(LEAVES, BLOCK, 128),
            bf16(LEAVES, LEAF, 128),
            pltpu.SemaphoreType.DMA((6,)),
        ],
        compiler_params=vmem(32),
        cost_estimate=cost(2 * 200 * 65536 * 272, 8 * MIB, 200 * 65536),
        name="remote_pairs",
    )(lists, arrived, left, right, own, field)


def turned(skel_ref, pair):
    return skel_ref[:, pl.ds(pair * 2 * RANK, 2 * RANK)].astype(jnp.float32).T


def field_pair(targets, blocks, halves):
    half_of = lax.broadcasted_iota(jnp.int32, (NRHS, 2 * RANK), 1) >> 6
    total = None
    for i, padded in enumerate((upper, below)):
        target = targets[i * RANK : (i + 1) * RANK]
        target_sq = jnp.sum(target * target, axis=1, keepdims=True) * 2
        source = jnp.concatenate([block[:DIM] for block in blocks[i]], axis=1)
        coeffs = jnp.concatenate(
            [
                jnp.where(half_of == half, block[DIM:], 0)
                for block, half in zip(blocks[i], halves[i], strict=True)
            ],
            axis=1,
        )
        wide = source.astype(jnp.float32)
        source_sq = jnp.sum(wide * wide, axis=0, keepdims=True) * 2
        power = dot((target * 4).astype(jnp.bfloat16), source) - target_sq - source_sq
        weights = jnp.exp(power).astype(jnp.bfloat16)
        term = dot(coeffs, padded(weights), NT)
        total = term if i == 0 else total + term
    return total


def far_one_kernel(
    far_ref, low_ref, arrived_ref, skel_hbm, near_hbm, one_hbm, out_ref, near_ref, one_ref, skel_ref,
    in_sem,
):
    copy, *brought = fetch(in_sem, (skel_hbm, skel_ref), (near_hbm, near_ref), (one_hbm, one_ref))
    copy.wait()
    for pair in range(PAIRS):
        clusters = (2 * pair, 2 * pair + 1)
        blocks = [
            [arrived_ref[far_ref[c, j] >> 3, :ROWS, :] for j in range(FAR)] for c in clusters
        ]
        halves = [
            [
                ((far_ref[c, j] & 7) != low_ref[0, far_ref[c, j] >> 3]).astype(jnp.int32)
                for j in range(FAR)
            ]
            for c in clusters
        ]
        out_ref[pair] = field_pair(turned(skel_ref, pair), blocks, halves)
    for copy in brought:
        copy.wait()


def far_one_field(far_one, low, arrived, skeleton_one, near, transfer_one):
    return pl.pallas_call(
        far_one_kernel,
        out_shape=(
            jax.ShapeDtypeStruct((PAIRS, NRHS, 2 * RANK), jnp.float32),
            jax.ShapeDtypeStruct(near.shape, near.dtype),
            jax.ShapeDtypeStruct(transfer_one.shape, transfer_one.dtype),
        ),
        in_specs=[SM, SM, VM, ANY, ANY, ANY],
        out_specs=(VM, VM, VM),
        scratch_shapes=[bf16(DIM, ONE * RANK), pltpu.SemaphoreType.DMA((3,))],
        compiler_params=vmem(16),
        cost_estimate=cost(1 << 28, 2 * MIB, 1 << 19),
        name="far_one_field",
    )(far_one, low, arrived, skeleton_one, near, transfer_one)


def final_kernel(
    far_ref, mine_ref, theirs_ref, field_one_ref, near_ref, one_ref, skel_hbm, two_hbm, basis_hbm,
    out_ref, skel_ref, two_ref, basis_ref, in_sem,
):
    core = lax.rem(lax.axis_index("leaf"), 2)
    skel_copy, two_copy, basis_copy = fetch(
        in_sem, (skel_hbm, skel_ref), (two_hbm, two_ref), (basis_hbm, basis_ref)
    )

    def split(x):
        high = x.astype(jnp.bfloat16)
        return jnp.concatenate([high, (x - high.astype(jnp.float32)).astype(jnp.bfloat16)], axis=0)

    def exact(parts, b):
        both = dot(parts, b)
        return both[:NRHS] + both[NRHS:]

    def whole(e, j):
        b = far_ref[e, j]
        rows = jnp.where((b & 1) == core, mine_ref[b >> 1], theirs_ref[b >> 1]).astype(jnp.float32)
        return jnp.concatenate([rows, pltpu.roll(rows, RANK, 1)], axis=0).astype(jnp.bfloat16)

    blocks = [[whole(e, j) for j in range(FAR)] for e in range(TWO)]
    skel_copy.wait()
    field_two = split(field_pair(turned(skel_ref, 0), blocks, [[0] * FAR] * TWO))
    two_copy.wait()
    from_two = [
        exact(field_two, padded(two_ref[e])) for e, padded in enumerate((upper, below))
    ]
    down_leaf = []
    for pair in range(PAIRS):
        parent = from_two[pair // 2][:, (pair % 2) * 2 * RANK : (pair % 2 + 1) * 2 * RANK]
        down_one = split(field_one_ref[pair] + parent)
        for i, padded in enumerate((upper, below)):
            down_leaf.append(exact(down_one, padded(one_ref[2 * pair + i])).astype(jnp.bfloat16))
    basis_copy.wait()
    for leaf in range(LEAVES):
        columns = pl.ds(leaf * LEAF, LEAF)
        at = (leaf % 4) // 2
        half = down_leaf[leaf // 4][:, at * 2 * RANK : (at + 1) * 2 * RANK]
        basis = (upper, below)[leaf % 2](basis_ref[:, columns])
        out_ref[:, columns] = (near_ref[:, columns] + dot(half, basis)).astype(jnp.bfloat16)


def finish(far_two, mine, theirs, field_one, near, transfer_one, *arrays):
    return pl.pallas_call(
        final_kernel,
        out_shape=jax.ShapeDtypeStruct((NRHS, LEAVES * LEAF), jnp.bfloat16),
        in_specs=[SM] + [VM] * 5 + [ANY] * 3,
        out_specs=VM,
        scratch_shapes=[bf16(*a.shape) for a in arrays] + [pltpu.SemaphoreType.DMA((3,))],
        compiler_params=vmem(16),
        cost_estimate=cost(1 << 28, 3 * MIB, 1 << 17),
        name="finish",
    )(far_two, mine, theirs, field_one, near, transfer_one, *arrays)


def shift(x, step):
    return lax.ppermute(x, "leaf", [(i, (i + step) % PEERS) for i in range(PEERS)])


def swap(x):
    return lax.ppermute(x, "leaf", [(i, i ^ 1) for i in range(PEERS)])


def exchange(x):
    return lax.all_to_all(x, "leaf", split_axis=0, concat_axis=0, tiled=True)


def local(
    points, rhs, basis, transfer_one, transfer_two, skeleton_one, skeleton_two, near_source,
    far_one, far_two,
):
    me = lax.axis_index("leaf")
    message, to_right, to_left, own, low = pack(
        near_source, far_one, skeleton_two, points, rhs
    )
    arrived = exchange(message)
    columns = coefficients(rhs, basis, transfer_one, transfer_two, skeleton_one, skeleton_two)
    field, lists = own_pairs(table_rows(near_source, me), own)
    to_right, to_left, columns, field, lists = lax.optimization_barrier(
        (to_right, to_left, columns, field, lists)
    )
    from_left, from_right = shift(to_right, 1), shift(to_left, -1)
    arrived, from_left, from_right = lax.optimization_barrier((arrived, from_left, from_right))
    far_arrived = exchange(far_pack(arrived, columns))
    near = remote_pairs(lists, arrived, from_left, from_right, own, field)
    far_arrived, near = lax.optimization_barrier((far_arrived, near))
    mine = jnp.concatenate([arrived[:, NEAR_MESSAGE - 8 :], far_arrived[:, ROWS:]], axis=1)
    theirs = swap(mine)
    near = pltpu.with_memory_space_constraint(near, pltpu.HBM)
    transfer_one = pltpu.with_memory_space_constraint(transfer_one, pltpu.HBM)
    field_one, near, transfer_one = far_one_field(
        far_one, low, far_arrived, skeleton_one, near, transfer_one
    )
    return finish(
        far_two, mine, theirs, field_one, near, transfer_one, skeleton_two, transfer_two, basis
    )


def solution(mesh):
    placed = (
        P(None, "leaf"),
        P(None, "leaf"),
        P(None, "leaf"),
        P("leaf", None, None),
        P("leaf", None, None),
        P(None, "leaf"),
        P(None, "leaf"),
        P(),
        P("leaf", None),
        P("leaf", None),
    )
    return jax.shard_map(
        local, mesh=mesh, in_specs=placed, out_specs=P(None, "leaf"), check_vma=False
    )
```
